128 devices in a mesh: seq: 8 (over z, x_lo), res: 16 (over x_hi, y, core).
Axes of the slice: x: 4 (x_hi: 2, x_lo: 2; x = x_hi * 2 + x_lo), y: 4, z: 4, core: 2. Of those that a mesh axis runs over, the one named last changes fastest.
Arguments:
- alignment_rows: bfloat16 [64, 1024, 256], P('seq', 'res'), may hold values from -6 to 6
- pair_entries: bfloat16 [1024, 1024, 128], P('res', 'seq'), may hold values from -6 to 6
- combined_weight: bfloat16 [256, 1024], replicated, may hold values from -0.375 to 0.375
- output_weight: bfloat16 [256, 256], replicated, may hold values from -0.375 to 0.375
- pair_weight: float32 [128, 8], replicated, may hold values from -9 to 9
- updated_gradient: bfloat16 [64, 1024, 256], P('seq', 'res'), may hold values from -6 to 6
Outputs:
- updated: bfloat16 [64, 1024, 256], P('seq', 'res')
- alignment_gradient: bfloat16 [64, 1024, 256], P('seq', 'res')
- pair_gradient: bfloat16 [1024, 1024, 128], P('res', 'seq')
- combined_weight_gradient: float32 [256, 1024], replicated
- output_weight_gradient: float32 [256, 256], replicated
- pair_weight_gradient: float32 [128, 8], replicated
The draws below stay inside these ranges and needn't reach their ends.
All inputs are finite; a program needn't handle non-finite values.
Results may differ from the reference program's by a relative error of at most 0.011.
Values may be sent and summed in bfloat16 or wider, within the bound.
A program may use at most 128 MiB of HBM per device.

```python
import math
import jax
import jax.numpy as jnp
from jax import lax

ALIGNMENT_WIDTH = 256
PAIR_WIDTH = 128
HEAD_COUNT = 8
HEAD_DIM = 32
QUERY_CHANNELS = 256
SEQUENCE_TOTAL = 64
RESIDUE_TOTAL = 1024


def shared_pair(key):
    basis_rows = jnp.clip(jax.random.normal(jax.random.fold_in(key, 5), (PAIR_WIDTH, HEAD_COUNT), jnp.float32), -5.0, 5.0)
    return basis_rows


def draw_pair_weight(key, part):
    basis_rows = shared_pair(key)
    drawn = basis_rows / math.sqrt(PAIR_WIDTH)
    return drawn


def draw_pair_entries(key, part):
    key = jax.random.fold_in(key, 22)
    noise_draw = jnp.clip(jax.random.normal(jax.random.fold_in(key, 1), (RESIDUE_TOTAL, RESIDUE_TOTAL, PAIR_WIDTH), jnp.float32), -6.0, 6.0)
    return noise_draw.astype(jnp.bfloat16)


def levels(own_key, extent, split, low, top_value):
    def one(dim, blocks):
        heights = jax.random.uniform(jax.random.fold_in(jax.random.fold_in(own_key, 6), dim), (blocks,), jnp.float32, low / len(split), top_value / len(split))
        return jnp.repeat(jnp.exp(heights), extent[dim] // blocks).reshape((-1,) + (1,) * (len(extent) - dim - 1))

    loudness = one(*split[0])
    for cut in split[1:]:
        loudness = loudness * one(*cut)
    return loudness


def gaussian(own_key, shape, deviation, reach, shards=(), kind=jnp.bfloat16):
    factor_of = levels(own_key, shape, shards, -0.22, 0.18) if shards else 1.0
    result = jax.random.normal(own_key, shape, jnp.float32) * deviation * factor_of
    return jnp.minimum(jnp.maximum(result, -reach), reach).astype(kind)


def setup_inputs(seed: int = 0) -> dict:
    streams_of = jax.random.split(jax.random.key(seed), 7)
    return {
        "alignment_rows": gaussian(streams_of[0], (SEQUENCE_TOTAL, RESIDUE_TOTAL, ALIGNMENT_WIDTH), 1.0, 6.0, ((0, 8), (1, 16))),
        "pair_entries": draw_pair_entries(jax.random.fold_in(streams_of[6], 71), 0),
        "combined_weight": gaussian(streams_of[2], (ALIGNMENT_WIDTH, 4 * QUERY_CHANNELS), ALIGNMENT_WIDTH ** -0.5, 0.375),
        "output_weight": gaussian(streams_of[3], (QUERY_CHANNELS, ALIGNMENT_WIDTH), QUERY_CHANNELS ** -0.5, 0.375),
        "pair_weight": draw_pair_weight(jax.random.fold_in(streams_of[6], 71), 0),
        "updated_gradient": gaussian(streams_of[5], (SEQUENCE_TOTAL, RESIDUE_TOTAL, ALIGNMENT_WIDTH), 1.0, 6.0, ((0, 8), (1, 16))),
    }


eps_norm = 1e-05

def layer_normalize(values):
    values = values.astype(jnp.float32)
    center = values - lax.optimization_barrier(jnp.mean(values, axis=-1, keepdims=True))
    broadcast_pair = lax.rsqrt(lax.optimization_barrier(jnp.mean(center * center, axis=-1, keepdims=True)) + eps_norm)
    return (center * broadcast_pair, broadcast_pair)

def layer_norm_backward(normalized_gradient, normalized_rows, broadcast_pair):
    mean_grad = lax.optimization_barrier(jnp.mean(normalized_gradient, axis=-1, keepdims=True))
    mean_cross = lax.optimization_barrier(jnp.mean(normalized_gradient * normalized_rows, axis=-1, keepdims=True))
    return broadcast_pair * (normalized_gradient - mean_grad - normalized_rows * mean_cross)

def split_heads(tensor):
    return tensor.reshape(tensor.shape[0], tensor.shape[1], HEAD_COUNT, HEAD_DIM).astype(jnp.float32)

def lowered(tensor):
    return lax.optimization_barrier(tensor.astype(jnp.bfloat16)).astype(jnp.float32)

def reference(alignment_rows, pair_entries, combined_weight, output_weight, pair_weight, updated_gradient):
    token_count = SEQUENCE_TOTAL * RESIDUE_TOTAL
    query_width = QUERY_CHANNELS
    score_scale = 1.0 / math.sqrt(HEAD_DIM * SEQUENCE_TOTAL)
    normalized_rows, broadcast_pair = layer_normalize(alignment_rows)
    normalized_rows_backward = normalized_rows.astype(jnp.bfloat16).reshape(token_count, ALIGNMENT_WIDTH)
    projected = jnp.dot(normalized_rows_backward, combined_weight, preferred_element_type=jnp.float32).reshape(SEQUENCE_TOTAL, RESIDUE_TOTAL, 4 * query_width)
    queries = (projected[..., :query_width] * score_scale).astype(jnp.bfloat16)
    key_rows = projected[..., query_width:2 * query_width].astype(jnp.bfloat16)
    value_rows = projected[..., 2 * query_width:3 * query_width].astype(jnp.bfloat16)
    gate_open = jax.nn.sigmoid(projected[..., 3 * query_width:])
    pair_normed, pair_spread = layer_normalize(pair_entries)
    pair_bias = jnp.einsum('ijc,ch->hij', pair_normed, pair_weight, precision=lax.Precision.HIGHEST)
    logits = jnp.einsum('sihd,sjhd->hij', split_heads(queries), split_heads(key_rows)) + pair_bias
    row_top = lax.optimization_barrier(jnp.max(logits, axis=-1, keepdims=True))
    lifted = jnp.exp(logits - row_top)
    softmax_out = lifted / lax.optimization_barrier(jnp.sum(lifted, axis=-1, keepdims=True))
    softmax_low = lowered(softmax_out)
    attended = jnp.einsum('hij,sjhd->sihd', softmax_low, split_heads(value_rows)).reshape(SEQUENCE_TOTAL, RESIDUE_TOTAL, query_width)
    gated_out = (gate_open * attended).astype(jnp.bfloat16)
    flattened_gated = gated_out.reshape(token_count, query_width)
    updated = jnp.dot(flattened_gated, output_weight, preferred_element_type=jnp.float32).astype(jnp.bfloat16).reshape(SEQUENCE_TOTAL, RESIDUE_TOTAL, ALIGNMENT_WIDTH)
    flattened_gradient = updated_gradient.reshape(token_count, ALIGNMENT_WIDTH)
    grad_gated = jnp.dot(flattened_gradient, output_weight.T, preferred_element_type=jnp.float32).reshape(SEQUENCE_TOTAL, RESIDUE_TOTAL, query_width)
    output_weight_gradient = jnp.dot(flattened_gated.T, flattened_gradient, preferred_element_type=jnp.float32)
    grad_attended = (grad_gated * gate_open).astype(jnp.bfloat16)
    grad_gate_logit = grad_gated * attended * gate_open * (1.0 - gate_open)
    grad_probs = jnp.einsum('sihd,sjhd->hij', split_heads(grad_attended), split_heads(value_rows))
    row_dot = lax.optimization_barrier(jnp.sum(softmax_out * grad_probs, axis=-1, keepdims=True))
    grad_logits = softmax_out * (grad_probs - row_dot)
    grad_logits_b = lowered(grad_logits)
    grad_queries = jnp.einsum('hij,sjhd->sihd', grad_logits_b, split_heads(key_rows)) * score_scale
    grad_keys = jnp.einsum('hij,sihd->sjhd', grad_logits_b, split_heads(queries))
    grad_values = jnp.einsum('hij,sihd->sjhd', softmax_low, split_heads(grad_attended))
    projected_gradient = jnp.concatenate([grad_queries.reshape(SEQUENCE_TOTAL, RESIDUE_TOTAL, query_width), grad_keys.reshape(SEQUENCE_TOTAL, RESIDUE_TOTAL, query_width), grad_values.reshape(SEQUENCE_TOTAL, RESIDUE_TOTAL, query_width), grad_gate_logit], axis=-1).astype(jnp.bfloat16).reshape(token_count, 4 * query_width)
    combined_weight_gradient = jnp.dot(normalized_rows_backward.T, projected_gradient, preferred_element_type=jnp.float32)
    normalized_gradient = jnp.dot(projected_gradient, combined_weight.T, preferred_element_type=jnp.float32).reshape(SEQUENCE_TOTAL, RESIDUE_TOTAL, ALIGNMENT_WIDTH)
    alignment_gradient = layer_norm_backward(normalized_gradient, normalized_rows, broadcast_pair).astype(jnp.bfloat16)
    pair_weight_gradient = jnp.einsum('ijc,hij->ch', pair_normed, grad_logits, precision=lax.Precision.HIGHEST)
    grad_pair_normed = jnp.einsum('hij,ch->ijc', grad_logits, pair_weight, precision=lax.Precision.HIGHEST)
    pair_gradient = layer_norm_backward(grad_pair_normed, pair_normed, pair_spread).astype(jnp.bfloat16)
    return (updated, alignment_gradient, pair_gradient, combined_weight_gradient, output_weight_gradient, pair_weight_gradient)
```

```python
import math

import jax
import jax.numpy as jnp
from jax import lax
from jax.experimental import pallas as pl
from jax.experimental.pallas import tpu as pltpu
from jax.sharding import PartitionSpec as P

MESH = pl.DeviceIdType.MESH
EPS = 1e-05
SCALE = 1.0 / math.sqrt(2048)
F32 = jnp.float32
BF16 = jnp.bfloat16

IN_QA, IN_KV, GY, GX, GS, GF = 0, 8, 16, 48, 56, 64
PB_A, PB_Y, STAT = 72, 80, 84
OY, OS, OX, RT_A, RT_K = 88, 120, 128, 136, 144
DL_Y, DL_A = 152, 156
T_C, T_S, T_X, T_Y, T_AS, T_AC = 164, 165, 173, 174, 178, 186
SEM_COUNT = 187


def nt(a, b):
    return lax.dot_general(a, b, (((1,), (1,)), ((), ())), preferred_element_type=F32)


def tn(a, b):
    return lax.dot_general(a, b, (((0,), (0,)), ((), ())), preferred_element_type=F32)


def nn(a, b):
    return jnp.dot(a, b, preferred_element_type=F32)


def split2(v):
    hi = v.astype(BF16)
    lo = (v - hi.astype(F32)).astype(BF16)
    return hi, lo


def split3(v):
    hi = v.astype(BF16)
    rest = v - hi.astype(F32)
    mid = rest.astype(BF16)
    lo = (rest - mid.astype(F32)).astype(BF16)
    return hi, mid, lo


def kernel(
    al, pe, cw, ow, pwt, ug,
    upd, alg, pg, dcw, dow, dpw,
    nf, spb, nb, nbt, gate, gg, heads4, sb, qa, kv,
    xn, rst, bs, pb, bi, bt, st, lt, dpt, oa, okv, ra, rsb, xb, rx, rb, ret,
    dl, dr, dx, dpj, ch, chr_, ch2, chs, chx, chy, chf, pwacc,
    ssem, rsem,
):
    s = lax.axis_index("seq")
    r = lax.axis_index("res")
    z, xl = s // 2, s % 2
    xh, y, c = r // 8, (r // 2) % 4, r % 2
    p = xh * 2 + c

    def at_seq(k):
        return {"seq": ((z + k // 2) % 4) * 2 + (xl + k) % 2}

    def from_seq(k):
        return {"seq": ((z + 4 - k // 2) % 4) * 2 + (xl + k) % 2}

    def at_y(d):
        return {"res": xh * 8 + ((y + d) % 4) * 2 + c}

    at_x = {"res": (1 - xh) * 8 + y * 2 + c}
    at_c = {"res": xh * 8 + y * 2 + (1 - c)}

    def send(src, dst, i, where):
        return pltpu.make_async_remote_copy(
            src_ref=src, dst_ref=dst, send_sem=ssem.at[i], recv_sem=rsem.at[i],
            device_id=where, device_id_type=MESH,
        )

    bar = pltpu.get_barrier_semaphore()
    for k in range(1, 8):
        pl.semaphore_signal(bar, inc=1, device_id=at_seq(k), device_id_type=MESH)
    for d in range(1, 4):
        pl.semaphore_signal(bar, inc=1, device_id=at_y(d), device_id_type=MESH)
    pl.semaphore_signal(bar, inc=1, device_id=at_x, device_id_type=MESH)
    pl.semaphore_signal(bar, inc=1, device_id=at_c, device_id_type=MESH)

    def c_in_qa(k):
        return send(sb.at[at_seq(k)["seq"], pl.ds(0, 2)], qa.at[k, y], IN_QA + k, at_seq(k))

    def c_in_kv(k):
        return send(sb.at[at_seq(k)["seq"], pl.ds(2, 2)], kv.at[k, p], IN_KV + k, at_seq(k))

    def c_gy(k, d):
        return send(qa.at[k, y], qa.at[k, y], GY + k * 4 + d, at_y(d))

    def c_gx(k):
        return send(kv.at[k, p], kv.at[k, p], GX + k, at_x)

    def c_gs(k):
        return send(kv.at[k, p], kv.at[k, p], GS + k, at_c)

    px = (1 - xh) * 2 + c

    def c_gf(k):
        return send(kv.at[k, px], kv.at[k, px], GF + k, at_c)

    def c_pa(k):
        return send(bs.at[at_seq(k)["seq"]], pb.at[s // 4, s % 4], PB_A + k, at_seq(k))

    def c_py(d):
        return send(pb.at[:, (y + d) % 4], bi.at[y], PB_Y + d, at_y(d))

    def c_st(d):
        return send(st.at[y], st.at[y], STAT + d, at_y(d))

    def c_oy(k, d):
        return send(oa.at[k, (y + d) % 4], ra.at[k, d], OY + k * 4 + d, at_y(d))

    def c_os(k):
        return send(okv.at[k, 1 - c], rsb.at[k], OS + k, at_c)

    def c_ox(k):
        return send(xb.at[k], rx.at[k], OX + k, at_x)

    def c_ra(k):
        return send(rb.at[k, pl.ds(0, 2)], ret.at[s, pl.ds(0, 2)], RT_A + k, from_seq(k))

    def c_rk(k):
        return send(rb.at[k, pl.ds(2, 2)], ret.at[s, pl.ds(2, 2)], RT_K + k, from_seq(k))

    def c_dy(d):
        return send(dl.at[(y + d) % 4], dr.at[:, y], DL_Y + d, at_y(d))

    def c_da(k):
        w = at_seq(k)["seq"]
        return send(dr.at[w // 4, w % 4], dx.at[s], DL_A + k, at_seq(k))

    def c_tc():
        return send(ch.at[1 - c], chr_, T_C, at_c)

    def c_ts(k):
        return send(ch2.at[at_seq(k)["seq"]], chs.at[k], T_S + k, at_seq(k))

    def c_tx():
        return send(chs.at[0], chx.at[0], T_X, at_x)

    def c_ty(d):
        return send(chx.at[1], chy.at[d], T_Y + d, at_y(d))

    def c_as(k):
        return send(chf.at[c, s], chf.at[c, s], T_AS + k, at_seq(k))

    def c_ac():
        return send(chf.at[c], chf.at[c], T_AC, at_c)

    for q in range(8):
        x = al[q].astype(F32)
        cen = x - jnp.mean(x, axis=-1, keepdims=True)
        spread = lax.rsqrt(jnp.mean(cen * cen, axis=-1, keepdims=True) + EPS)
        normed = cen * spread
        rows = pl.ds(q * 64, 64)
        nf[rows, :] = normed
        spb[rows, :] = jnp.broadcast_to(spread, (64, 128))
        nb[rows, :] = normed.astype(BF16)
    for q in range(8):
        rows = pl.ds(q * 64, 64)
        n = nb[rows, :]
        heads4[0, q] = (nn(n, cw[:, 0:256]) * SCALE).astype(BF16)
        heads4[2, q] = nn(n, cw[:, 256:512]).astype(BF16)
        heads4[3, q] = nn(n, cw[:, 512:768]).astype(BF16)
        open_ = 1.0 / (1.0 + jnp.exp(-nn(n, cw[:, 768:1024])))
        gate[rows, :] = open_
        grad = nt(ug[q], ow[...])
        gg[rows, :] = grad
        heads4[1, q] = (grad * open_).astype(BF16)
    for h in range(8):
        for t in range(4):
            sb[h, t] = jnp.concatenate(
                [heads4[t, q][:, h * 32:(h + 1) * 32] for q in range(8)], axis=-1
            )

    pl.semaphore_wait(bar, 12)

    def start_in(k, _):
        c_in_qa(k).start()
        c_in_kv(k).start()
        return 0

    lax.fori_loop(1, 8, start_in, 0)
    qa[0, y] = sb[s, 0:2]
    kv[0, p] = sb[s, 2:4]

    def forward(k):
        for d in (1, 3, 2):
            c_gy(k, d).start()
        c_gx(k).start()
        c_gs(k).start()

    ones = jnp.ones((128, 128), BF16)
    w_all = pwt[...]
    w3 = jnp.concatenate(split3(w_all), axis=0)

    def pair_chunk(k):
        base = pl.multiple_of(k * 1024, 1024)
        x = pe[pl.ds(k * 8, 8)].reshape(1024, 128)
        cen = x.astype(F32) - nn(x, ones) * (1.0 / 128)
        hi, lo = split2(cen * cen)
        spread = lax.rsqrt((nn(hi, ones) + nn(lo, ones)) * (1.0 / 128) + EPS)
        normed = cen * spread
        xn[pl.ds(base, 1024), :] = normed
        rst[pl.ds(base, 1024), :] = spread
        hi, lo = split2(normed)
        b = nt(w3, hi) + nt(w3, lo)
        b = b[0:8] + b[8:16] + b[16:24]
        for q in range(8):
            bs[:, k * 8 + q, :] = b[:, q * 128:(q + 1) * 128]

    forward(0)
    pair_chunk(0)

    def stage_in(k, _):
        c_in_qa(k).wait_recv()
        c_in_kv(k).wait_recv()
        forward(k)
        c_gx(k - 1).wait_recv()
        c_gf(k - 1).start()
        pair_chunk(k)
        return 0

    lax.fori_loop(1, 8, stage_in, 0)
    c_gx(7).wait_recv()
    c_gf(7).start()

    def start_pair(k, _):
        c_pa(k).start()
        return 0

    lax.fori_loop(1, 8, start_pair, 0)
    pb[s // 4, s % 4] = bs[s]
    nbt[...] = nb[...].T

    def wait_pair(k, _):
        c_pa(k).wait_recv()
        return 0

    lax.fori_loop(1, 8, wait_pair, 0)
    for d in range(1, 4):
        c_py(d).start()
    bi[y] = pb[:, y]

    lt[...] = jnp.zeros_like(lt)
    dpt[...] = jnp.zeros_like(dpt)

    def stage_mm(k, _):
        for d in range(1, 4):
            c_gy(k, d).wait_recv()
        c_gs(k).wait_recv()
        c_gf(k).wait_recv()
        qk = qa[k, :, 0].reshape(256, 256)
        dak = qa[k, :, 1].reshape(256, 256)
        kk = kv[k, :, 0].reshape(256, 256)
        vk = kv[k, :, 1].reshape(256, 256)
        lt[...] += nt(kk, qk)
        dpt[...] += nt(vk, dak)
        return 0

    lax.fori_loop(0, 8, stage_mm, 0)
    for d in range(1, 4):
        c_py(d).wait_recv()
    bias = jnp.concatenate(
        [jnp.concatenate([bi[a, b] for a in range(4)], axis=0) for b in range(2)], axis=1
    )
    logits = lt[...] + bias.T
    top = jnp.max(logits, axis=0, keepdims=True)
    e = jnp.exp(logits - top)
    dp = dpt[...]
    total = jnp.sum(e, axis=0, keepdims=True)
    dots = jnp.sum(e * dp, axis=0, keepdims=True)
    st[y] = jnp.concatenate([top, total, dots, jnp.zeros((5, 256), F32)], axis=0)
    for d in range(1, 4):
        c_st(d).start()
    lt[...] = e
    for d in range(1, 4):
        c_st(d).wait_recv()
    stats = [st[a] for a in range(4)]
    peak = jnp.maximum(
        jnp.maximum(stats[0][0:1], stats[1][0:1]), jnp.maximum(stats[2][0:1], stats[3][0:1])
    )
    z_sum = jnp.zeros((1, 256), F32)
    d_sum = jnp.zeros((1, 256), F32)
    for a in range(4):
        f = jnp.exp(stats[a][0:1] - peak)
        z_sum += f * stats[a][1:2]
        d_sum += f * stats[a][2:3]
    inv = 1.0 / z_sum
    mine = st[y]
    prob_t = lt[...] * (jnp.exp(mine[0:1] - peak) * inv)
    grad_t = prob_t * (dpt[...] - d_sum * inv)
    lt[...] = prob_t
    dpt[...] = grad_t
    grad = grad_t.T
    for a in range(4):
        for b in range(2):
            dl[a, b] = grad[a * 64:(a + 1) * 64, b * 128:(b + 1) * 128]
    for d in range(1, 4):
        c_dy(d).start()
    dr[:, y] = dl[y]
    bt[0] = lt[...].astype(BF16)
    bt[1] = bt[0].T
    bt[2] = dpt[...].astype(BF16)
    bt[3] = grad.astype(BF16)

    def stage_out(k):
        qk = qa[k, :, 0].reshape(256, 256)
        dak = qa[k, :, 1].reshape(256, 256)
        kk = kv[k, :, 0].reshape(256, 256)
        vk = kv[k, :, 1].reshape(256, 256)
        oa[k, :, 0] = nn(bt[1], vk).astype(BF16).reshape(4, 64, 256)
        oa[k, :, 1] = (nn(bt[3], kk) * SCALE).astype(BF16).reshape(4, 64, 256)
        for d in (1, 3, 2):
            c_oy(k, d).start()
        dk = nn(bt[2], qk).astype(BF16)
        dv = nn(bt[0], dak).astype(BF16)
        for a in range(2):
            for b in range(2):
                at = (a * 2 + b) * 64
                okv[k, b, a, 0] = dk[at:at + 64]
                okv[k, b, a, 1] = dv[at:at + 64]
        c_os(k).start()

    def stage_x(k):
        c_os(k).wait_recv()
        xb[k] = (okv[k, c, 1 - xh].astype(F32) + rsb[k, 1 - xh].astype(F32)).astype(BF16)
        c_ox(k).start()

    def loop_out(i, _):
        stage_out((i + 1) % 8)
        return 0

    lax.fori_loop(0, 8, loop_out, 0)

    def loop_x(i, _):
        stage_x((i + 1) % 8)
        return 0

    lax.fori_loop(0, 8, loop_x, 0)

    for d in range(1, 4):
        c_dy(d).wait_recv()

    def start_da(k, _):
        c_da(k).start()
        return 0

    lax.fori_loop(1, 8, start_da, 0)
    dx[s] = dr[s // 4, s % 4]

    def sums(k):
        for d in range(1, 4):
            c_oy(k, d).wait_recv()
        rb[k, 0:2] = (
            (oa[k, y].astype(F32) + ra[k, 1].astype(F32))
            + (ra[k, 2].astype(F32) + ra[k, 3].astype(F32))
        ).astype(BF16)
        c_ox(k).wait_recv()
        rb[k, 2:4] = (
            okv[k, c, xh].astype(F32) + rsb[k, xh].astype(F32) + rx[k].astype(F32)
        ).astype(BF16)

    def loop_sum(k, _):
        sums(k)
        c_ra(k).start()
        c_rk(k).start()
        return 0

    lax.fori_loop(1, 8, loop_sum, 0)
    sums(0)
    ret[s] = rb[0]

    def wait_ret(k, _):
        c_ra(k).wait_recv()
        c_rk(k).wait_recv()
        return 0

    lax.fori_loop(1, 8, wait_ret, 0)

    def unshuffle(t, q):
        return jnp.concatenate(
            [ret[h, t][:, q * 32:(q + 1) * 32] for h in range(8)], axis=-1
        )

    for q in range(8):
        rows = pl.ds(q * 64, 64)
        att = unshuffle(0, q).astype(F32)
        open_ = gate[rows, :]
        out = (open_ * att).astype(BF16)
        heads4[0, q] = out
        upd[q] = nn(out, ow[...]).astype(BF16)
        dpj[3, rows, :] = (gg[rows, :] * att * open_ * (1.0 - open_)).astype(BF16)
        for t in range(3):
            dpj[t, rows, :] = unshuffle(t + 1, q)
    for g in range(4):
        w = nn(nbt[...], dpj[g]).reshape(2, 8, 16, 256)
        ch[:, :, g * 16:(g + 1) * 16, :] = w
    w = tn(heads4[0].reshape(512, 256), ug[...].reshape(512, 256)).reshape(2, 8, 16, 256)
    ch[:, :, 64:80, :] = w

    def wait_da(k, _):
        c_da(k).wait_recv()
        return 0

    lax.fori_loop(1, 8, wait_da, 0)
    w_mean = jnp.mean(w_all, axis=-1, keepdims=True)
    v_hi, v_mid, _ = split3(w_all - w_mean)
    one_rows = jnp.where(
        lax.broadcasted_iota(jnp.int32, (8, 128), 0) < 2, 1.0, 0.0
    ).astype(BF16)
    zero_rows = jnp.zeros((8, 128), BF16)
    rhs = jnp.concatenate(
        [
            jnp.concatenate([v_hi, zero_rows], axis=1),
            jnp.concatenate([v_mid, zero_rows], axis=1),
            jnp.concatenate([v_hi, zero_rows], axis=1),
            jnp.concatenate([zero_rows, one_rows], axis=1),
        ],
        axis=0,
    )
    pwacc[...] = jnp.zeros_like(pwacc)

    def pair_back(k, _):
        base = pl.multiple_of(k * 1024, 1024)
        g = jnp.concatenate([dx[:, k * 8 + q, :] for q in range(8)], axis=1)
        b = jnp.concatenate([bs[:, k * 8 + q, :] for q in range(8)], axis=1)
        cross = jnp.sum(g * b, axis=0, keepdims=True) * (1.0 / 128)
        c_hi, c_lo = split2(cross)
        g_hi, g_lo = split2(g)
        tail = jnp.concatenate(
            [c_hi.astype(F32), c_lo.astype(F32), jnp.zeros((6, 1024), F32)], axis=0
        ).astype(BF16)
        lhs = jnp.concatenate([g_hi, g_hi, g_lo, tail], axis=0)
        both = tn(lhs, rhs)
        normed = xn[pl.ds(base, 1024), :]
        back = rst[pl.ds(base, 1024), :] * (both[:, 0:128] - normed * both[:, 128:256])
        pg[pl.ds(k * 8, 8)] = back.astype(BF16).reshape(8, 128, 128)
        n_hi, n_lo = split2(normed)
        g2 = jnp.concatenate([g_hi, g_lo], axis=0)
        part = nn(g2, n_hi) + nn(g2, n_lo)
        pwacc[...] += part[0:8] + part[8:16]
        return 0

    lax.fori_loop(0, 8, pair_back, 0)
    ch[:, :, 80:88, :] = jnp.zeros((2, 8, 8, 256), F32)
    ch[0, 0, 80:88, 0:128] = pwacc[...]

    c_tc().start()
    for q in range(8):
        rows = pl.ds(q * 64, 64)
        d = nt(dpj[0, rows, :], cw[:, 0:256])
        for g in range(1, 4):
            d += nt(dpj[g, rows, :], cw[:, g * 256:(g + 1) * 256])
        n = nf[rows, :]
        spread = spb[rows, 0:1]
        mean_d = jnp.mean(d, axis=-1, keepdims=True)
        mean_x = jnp.mean(d * n, axis=-1, keepdims=True)
        alg[q] = (spread * (d - mean_d - n * mean_x)).astype(BF16)
    c_tc().wait_recv()
    ch2[...] = ch[c] + chr_[...]

    def start_ts(k, _):
        c_ts(k).start()
        return 0

    lax.fori_loop(1, 8, start_ts, 0)
    acc = ch2[s]
    for k in range(1, 8):
        c_ts(k).wait_recv()
        acc += chs[k]
    chs[0] = acc
    c_tx().start()
    c_tx().wait_recv()
    acc += chx[0]
    chx[1] = acc
    for d in range(1, 4):
        c_ty(d).start()
    chy[0] = acc
    for d in range(1, 4):
        c_ty(d).wait_recv()
    acc = jnp.zeros((88, 256), F32)
    for a in range(4):
        acc += chy[(y + 4 - a) % 4]
    chf[c, s] = acc

    def start_as(k, _):
        c_as(k).start()
        return 0

    lax.fori_loop(1, 8, start_as, 0)
    for k in range(1, 8):
        c_as(k).wait_recv()
    c_ac().start()
    c_ac().wait_recv()
    for b in range(2):
        for q in range(8):
            at = (b * 8 + q) * 16
            for g in range(4):
                dcw[at:at + 16, g * 256:(g + 1) * 256] = chf[b, q, g * 16:(g + 1) * 16, :]
            dow[at:at + 16, :] = chf[b, q, 64:80, :]
    dpw[...] = chf[0, 0, 80:88, 0:128]

    def drain(k, _):
        c_in_qa(k).wait_send()
        c_in_kv(k).wait_send()
        c_pa(k).wait_send()
        c_ra(k).wait_send()
        c_rk(k).wait_send()
        c_da(k).wait_send()
        c_ts(k).wait_send()
        c_as(k).wait_send()
        return 0

    lax.fori_loop(1, 8, drain, 0)

    def drain_all(k, _):
        for d in range(1, 4):
            c_gy(k, d).wait_send()
            c_oy(k, d).wait_send()
        c_gx(k).wait_send()
        c_gs(k).wait_send()
        c_gf(k).wait_send()
        c_os(k).wait_send()
        c_ox(k).wait_send()
        return 0

    lax.fori_loop(0, 8, drain_all, 0)
    for d in range(1, 4):
        c_py(d).wait_send()
        c_st(d).wait_send()
        c_dy(d).wait_send()
        c_ty(d).wait_send()
    c_tc().wait_send()
    c_tx().wait_send()
    c_ac().wait_send()


def body(alignment_rows, pair_entries, combined_weight, output_weight, pair_weight, updated_gradient):
    V = pltpu.VMEM
    scratch = [
        V((512, 256), F32),
        V((512, 128), F32),
        V((512, 256), BF16),
        V((256, 512), BF16),
        V((512, 256), F32),
        V((512, 256), F32),
        V((4, 8, 64, 256), BF16),
        V((8, 4, 64, 256), BF16),
        V((8, 4, 2, 64, 256), BF16),
        V((8, 4, 2, 64, 256), BF16),
        V((8192, 128), F32),
        V((8192, 128), F32),
        V((8, 64, 128), F32),
        V((2, 4, 64, 128), F32),
        V((4, 2, 64, 128), F32),
        V((4, 256, 256), BF16),
        V((4, 8, 256), F32),
        V((256, 256), F32),
        V((256, 256), F32),
        V((8, 4, 2, 64, 256), BF16),
        V((8, 2, 2, 2, 64, 256), BF16),
        V((8, 4, 2, 64, 256), BF16),
        V((8, 2, 2, 64, 256), BF16),
        V((8, 2, 64, 256), BF16),
        V((8, 2, 64, 256), BF16),
        V((8, 4, 64, 256), BF16),
        V((8, 4, 64, 256), BF16),
        V((4, 2, 64, 128), F32),
        V((2, 4, 64, 128), F32),
        V((8, 64, 128), F32),
        V((4, 512, 256), BF16),
        V((2, 8, 88, 256), F32),
        V((8, 88, 256), F32),
        V((8, 88, 256), F32),
        V((8, 88, 256), F32),
        V((2, 88, 256), F32),
        V((4, 88, 256), F32),
        V((2, 8, 88, 256), F32),
        V((8, 128), F32),
        pltpu.SemaphoreType.DMA((SEM_COUNT,)),
        pltpu.SemaphoreType.DMA((SEM_COUNT,)),
    ]
    vm = pl.BlockSpec(memory_space=pltpu.VMEM)
    out = pl.pallas_call(
        kernel,
        out_shape=(
            jax.ShapeDtypeStruct((8, 64, 256), BF16),
            jax.ShapeDtypeStruct((8, 64, 256), BF16),
            jax.ShapeDtypeStruct((64, 128, 128), BF16),
            jax.ShapeDtypeStruct((256, 1024), F32),
            jax.ShapeDtypeStruct((256, 256), F32),
            jax.ShapeDtypeStruct((8, 128), F32),
        ),
        in_specs=[vm] * 6,
        out_specs=(vm,) * 6,
        scratch_shapes=scratch,
        compiler_params=pltpu.CompilerParams(
            collective_id=0, has_side_effects=True, vmem_limit_bytes=62 << 20
        ),
        name="row_attention",
    )(alignment_rows, pair_entries, combined_weight, output_weight, pair_weight.T, updated_gradient)
    return out[0], out[1], out[2], out[3], out[4], out[5].T


def solution(mesh):
    return jax.shard_map(
        body,
        mesh=mesh,
        in_specs=(
            P("seq", "res", None),
            P("res", "seq", None),
            P(),
            P(),
            P(),
            P("seq", "res", None),
        ),
        out_specs=(
            P("seq", "res", None),
            P("seq", "res", None),
            P("res", "seq", None),
            P(),
            P(),
            P(),
        ),
        check_vma=False,
    )
```

```python
import math

import jax
import jax.numpy as jnp
from jax import lax
from jax.experimental import pallas as pl
from jax.experimental.pallas import tpu as pltpu
from jax.sharding import PartitionSpec as P

MESH = pl.DeviceIdType.MESH
EPS = 1e-05
SCALE = 1.0 / math.sqrt(2048)
F32 = jnp.float32
BF16 = jnp.bfloat16

IN_QA, IN_KV, GY, GX, GS, GF = 0, 8, 16, 48, 56, 64
PB_A, PB_Y, STAT = 72, 80, 84
OY, OS, OX, RT_A, RT_K = 88, 120, 128, 136, 144
DL_Y, DL_A = 152, 156
T_C, T_S, T_XY, T_AS, T_AC = 164, 165, 173, 181, 189
SEM_COUNT = 190


def nt(a, b):
    return lax.dot_general(a, b, (((1,), (1,)), ((), ())), preferred_element_type=F32)


def tn(a, b):
    return lax.dot_general(a, b, (((0,), (0,)), ((), ())), preferred_element_type=F32)


def nn(a, b):
    return jnp.dot(a, b, preferred_element_type=F32)


def split2(v):
    hi = v.astype(BF16)
    lo = (v - hi.astype(F32)).astype(BF16)
    return hi, lo


def split3(v):
    hi = v.astype(BF16)
    rest = v - hi.astype(F32)
    mid = rest.astype(BF16)
    lo = (rest - mid.astype(F32)).astype(BF16)
    return hi, mid, lo


def kernel(
    al, pe_in, cw, ow, pw, ug,
    upd, alg, pg_out, chf,
    nf, spb, nb, nbt, gate, gg, heads4, sb, qa, kv,
    xn, rst, bs, pb, bi, bt, st, lt, dpt, oa, okv, ra, rsb, xb, rx, rb, ret,
    dl, dr, dx, dpj, ch, chr_, ch2, chs, chx, chy, pwacc,
    pe, pg, ssem, rsem, lsem,
):
    s = lax.axis_index("seq")
    r = lax.axis_index("res")
    z, xl = s // 2, s % 2
    xh, y, c = r // 8, (r // 2) % 4, r % 2
    p = xh * 2 + c

    def at_seq(k):
        return {"seq": ((z + k // 2) % 4) * 2 + (xl + k) % 2}

    def from_seq(k):
        return {"seq": ((z + 4 - k // 2) % 4) * 2 + (xl + k) % 2}

    def at_y(d):
        return {"res": xh * 8 + ((y + d) % 4) * 2 + c}

    def at_xy(m):
        return {"res": ((xh + m // 4) % 2) * 8 + ((y + m) % 4) * 2 + c}

    at_x = {"res": (1 - xh) * 8 + y * 2 + c}
    at_c = {"res": xh * 8 + y * 2 + (1 - c)}

    def send(src, dst, i, where):
        return pltpu.make_async_remote_copy(
            src_ref=src, dst_ref=dst, send_sem=ssem.at[i], recv_sem=rsem.at[i],
            device_id=where, device_id_type=MESH,
        )

    load = pltpu.make_async_copy(pe_in, pe, lsem.at[8])
    load.start()

    bar = pltpu.get_barrier_semaphore()
    for k in range(1, 8):
        pl.semaphore_signal(bar, inc=1, device_id=at_seq(k), device_id_type=MESH)
        pl.semaphore_signal(bar, inc=1, device_id=at_xy(k), device_id_type=MESH)
    pl.semaphore_signal(bar, inc=1, device_id=at_c, device_id_type=MESH)

    def c_in_qa(k):
        return send(sb.at[at_seq(k)["seq"], pl.ds(0, 2)], qa.at[k, y], IN_QA + k, at_seq(k))

    def c_in_kv(k):
        return send(sb.at[at_seq(k)["seq"], pl.ds(2, 2)], kv.at[k, p], IN_KV + k, at_seq(k))

    def c_gy(k, d):
        return send(qa.at[k, y], qa.at[k, y], GY + k * 4 + d, at_y(d))

    def c_gx(k):
        return send(kv.at[k, p], kv.at[k, p], GX + k, at_x)

    def c_gs(k):
        return send(kv.at[k, p], kv.at[k, p], GS + k, at_c)

    px = (1 - xh) * 2 + c

    def c_gf(k):
        return send(kv.at[k, px], kv.at[k, px], GF + k, at_c)

    def c_pa(k):
        return send(bs.at[at_seq(k)["seq"]], pb.at[s // 4, s % 4], PB_A + k, at_seq(k))

    def c_py(d):
        return send(pb.at[:, (y + d) % 4], bi.at[y], PB_Y + d, at_y(d))

    def c_st(d):
        return send(st.at[y], st.at[y], STAT + d, at_y(d))

    def c_oy(k, d):
        return send(oa.at[k, (y + d) % 4], ra.at[k, d], OY + k * 4 + d, at_y(d))

    def c_os(k):
        return send(okv.at[k, 1 - c], rsb.at[k], OS + k, at_c)

    def c_ox(k):
        return send(xb.at[k], rx.at[k], OX + k, at_x)

    def c_ra(k):
        return send(rb.at[k, pl.ds(0, 2)], ret.at[s, pl.ds(0, 2)], RT_A + k, from_seq(k))

    def c_rk(k):
        return send(rb.at[k, pl.ds(2, 2)], ret.at[s, pl.ds(2, 2)], RT_K + k, from_seq(k))

    def c_dy(d):
        return send(dl.at[(y + d) % 4], dr.at[:, y], DL_Y + d, at_y(d))

    def c_da(k):
        w = at_seq(k)["seq"]
        return send(dr.at[w // 4, w % 4], dx.at[s], DL_A + k, at_seq(k))

    def c_tc():
        return send(ch.at[1 - c], chr_, T_C, at_c)

    def c_ts(k):
        return send(ch2.at[at_seq(k)["seq"]], chs.at[k], T_S + k, at_seq(k))

    def c_txy(m):
        return send(chx, chy.at[xh * 4 + y], T_XY + m, at_xy(m))

    def c_as(k):
        return send(chf.at[c, s], chf.at[c, s], T_AS + k, at_seq(k))

    def c_ac():
        return send(chf.at[c], chf.at[c], T_AC, at_c)

    for q in range(8):
        x = al[q].astype(F32)
        cen = x - jnp.mean(x, axis=-1, keepdims=True)
        spread = lax.rsqrt(jnp.mean(cen * cen, axis=-1, keepdims=True) + EPS)
        normed = cen * spread
        rows = pl.ds(q * 64, 64)
        nf[rows, :] = normed
        spb[rows, :] = jnp.broadcast_to(spread, (64, 128))
        nb[rows, :] = normed.astype(BF16)
    def shuffle(t):
        for h in range(8):
            sb[h, t] = jnp.concatenate(
                [heads4[t, q][:, h * 32:(h + 1) * 32] for q in range(8)], axis=-1
            )

    for q in range(8):
        rows = pl.ds(q * 64, 64)
        n = nb[rows, :]
        heads4[0, q] = (nn(n, cw[:, 0:256]) * SCALE).astype(BF16)
        heads4[2, q] = nn(n, cw[:, 256:512]).astype(BF16)
        heads4[3, q] = nn(n, cw[:, 512:768]).astype(BF16)
        open_ = 1.0 / (1.0 + jnp.exp(-nn(n, cw[:, 768:1024])))
        gate[rows, :] = open_
        grad = nt(ug[q], ow[...])
        gg[rows, :] = grad
        heads4[1, q] = (grad * open_).astype(BF16)
    for h in range(8):
        for t in range(4):
            sb[h, t] = jnp.concatenate(
                [heads4[t, q][:, h * 32:(h + 1) * 32] for q in range(8)], axis=-1
            )
    pl.semaphore_wait(bar, 15)

    def start_in(k, _):
        c_in_qa(k).start()
        c_in_kv(k).start()
        return 0

    lax.fori_loop(1, 8, start_in, 0)
    qa[0, y] = sb[s, 0:2]
    kv[0, p] = sb[s, 2:4]
    c_gx(0).start()
    c_gs(0).start()
    for d in (1, 3, 2):
        c_gy(0, d).start()

    load.wait()
    ones = jnp.ones((128, 128), BF16)
    w_all = pw[...]
    w3 = jnp.concatenate(split3(w_all), axis=0)

    def pair_chunk(k):
        base = pl.multiple_of(k * 1024, 1024)
        x = pe[pl.ds(k * 8, 8)].reshape(1024, 128)
        cen = x.astype(F32) - nn(x, ones) * (1.0 / 128)
        hi, lo = split2(cen * cen)
        spread = lax.rsqrt((nn(hi, ones) + nn(lo, ones)) * (1.0 / 128) + EPS)
        normed = cen * spread
        xn[pl.ds(base, 1024), :] = normed
        rst[pl.ds(base, 1024), :] = spread
        hi, lo = split2(normed)
        b = nt(w3, hi) + nt(w3, lo)
        b = b[0:8] + b[8:16] + b[16:24]
        for q in range(8):
            bs[:, k * 8 + q, :] = b[:, q * 128:(q + 1) * 128]

    def stage_in(k, _):
        c_in_qa(k).wait_recv()
        for d in (1, 3, 2):
            c_gy(k, d).start()
        c_in_kv(k).wait_recv()
        c_gx(k).start()
        c_gs(k).start()
        pair_chunk(k)
        return 0

    lax.fori_loop(1, 8, stage_in, 0)
    pair_chunk(0)

    def start_pair(k, _):
        c_pa(k).start()
        return 0

    lax.fori_loop(1, 8, start_pair, 0)
    pb[s // 4, s % 4] = bs[s]

    def share_x(k, _):
        c_gx(k).wait_recv()
        c_gf(k).start()
        return 0

    lax.fori_loop(0, 8, share_x, 0)
    nbt[...] = nb[...].T

    def wait_pair(k, _):
        c_pa(k).wait_recv()
        return 0

    lax.fori_loop(1, 8, wait_pair, 0)
    for d in range(1, 4):
        c_py(d).start()
    bi[y] = pb[:, y]

    dpt[...] = jnp.zeros_like(dpt)
    for d in range(1, 4):
        c_py(d).wait_recv()
    bias = jnp.concatenate(
        [jnp.concatenate([bi[a, b] for a in range(4)], axis=0) for b in range(2)], axis=1
    )
    lt[...] = bias.T

    def stage_mm(k, _):
        for d in range(1, 4):
            c_gy(k, d).wait_recv()
        c_gs(k).wait_recv()
        c_gf(k).wait_recv()
        qk = qa[k, :, 0].reshape(256, 256)
        dak = qa[k, :, 1].reshape(256, 256)
        kk = kv[k, :, 0].reshape(256, 256)
        vk = kv[k, :, 1].reshape(256, 256)
        lt[...] += nt(kk, qk)
        dpt[...] += nt(vk, dak)
        return 0

    lax.fori_loop(0, 8, stage_mm, 0)
    logits = lt[...]
    top = jnp.max(logits, axis=0, keepdims=True)
    e = jnp.exp(logits - top)
    dp = dpt[...]
    total = jnp.sum(e, axis=0, keepdims=True)
    dots = jnp.sum(e * dp, axis=0, keepdims=True)
    st[y] = jnp.concatenate([top, total, dots, jnp.zeros((5, 256), F32)], axis=0)
    for d in range(1, 4):
        c_st(d).start()
    lt[...] = e
    for d in range(1, 4):
        c_st(d).wait_recv()
    stats = [st[a] for a in range(4)]
    peak = jnp.maximum(
        jnp.maximum(stats[0][0:1], stats[1][0:1]), jnp.maximum(stats[2][0:1], stats[3][0:1])
    )
    z_sum = jnp.zeros((1, 256), F32)
    d_sum = jnp.zeros((1, 256), F32)
    for a in range(4):
        f = jnp.exp(stats[a][0:1] - peak)
        z_sum += f * stats[a][1:2]
        d_sum += f * stats[a][2:3]
    inv = 1.0 / z_sum
    mine = st[y]
    prob_t = lt[...] * (jnp.exp(mine[0:1] - peak) * inv)
    grad_t = prob_t * (dpt[...] - d_sum * inv)
    lt[...] = prob_t
    dpt[...] = grad_t
    grad = grad_t.T
    for a in range(4):
        for b in range(2):
            dl[a, b] = grad[a * 64:(a + 1) * 64, b * 128:(b + 1) * 128]
    for d in range(1, 4):
        c_dy(d).start()
    dr[:, y] = dl[y]
    bt[0] = lt[...].astype(BF16)
    bt[1] = bt[0].T
    bt[2] = dpt[...].astype(BF16)
    bt[3] = grad.astype(BF16)

    def stage_out(k):
        qk = qa[k, :, 0].reshape(256, 256)
        dak = qa[k, :, 1].reshape(256, 256)
        kk = kv[k, :, 0].reshape(256, 256)
        vk = kv[k, :, 1].reshape(256, 256)
        oa[k, :, 0] = nn(bt[1], vk).astype(BF16).reshape(4, 64, 256)
        oa[k, :, 1] = (nn(bt[3], kk) * SCALE).astype(BF16).reshape(4, 64, 256)
        for d in (1, 3, 2):
            c_oy(k, d).start()
        dk = nn(bt[2], qk).astype(BF16)
        dv = nn(bt[0], dak).astype(BF16)
        for a in range(2):
            for b in range(2):
                at = (a * 2 + b) * 64
                okv[k, b, a, 0] = dk[at:at + 64]
                okv[k, b, a, 1] = dv[at:at + 64]
        c_os(k).start()

    def stage_x(k):
        c_os(k).wait_recv()
        xb[k] = (okv[k, c, 1 - xh].astype(F32) + rsb[k, 1 - xh].astype(F32)).astype(BF16)
        c_ox(k).start()

    stage_out(1)

    def loop_out(i, _):
        stage_out((i + 1) % 8)
        stage_x(i)
        return 0

    lax.fori_loop(1, 8, loop_out, 0)
    stage_x(0)

    for d in range(1, 4):
        c_dy(d).wait_recv()

    def start_da(k, _):
        c_da(k).start()
        return 0

    lax.fori_loop(1, 8, start_da, 0)
    dx[s] = dr[s // 4, s % 4]

    def wait_da(k, _):
        c_da(k).wait_recv()
        return 0

    lax.fori_loop(1, 8, wait_da, 0)
    w_mean = jnp.mean(w_all, axis=-1, keepdims=True)
    v_hi, v_mid, _ = split3(w_all - w_mean)
    one_rows = jnp.where(
        lax.broadcasted_iota(jnp.int32, (8, 128), 0) < 2, 1.0, 0.0
    ).astype(BF16)
    zero_rows = jnp.zeros((8, 128), BF16)
    rhs = jnp.concatenate(
        [
            jnp.concatenate([v_hi, zero_rows], axis=1),
            jnp.concatenate([v_mid, zero_rows], axis=1),
            jnp.concatenate([v_hi, zero_rows], axis=1),
            jnp.concatenate([zero_rows, one_rows], axis=1),
        ],
        axis=0,
    )
    pwacc[...] = jnp.zeros_like(pwacc)

    def store(k):
        rows = pl.ds(k * 8, 8)
        return pltpu.make_async_copy(pg.at[rows], pg_out.at[rows], lsem.at[k])

    def pair_back(k):
        base = pl.multiple_of(k * 1024, 1024)
        g = jnp.concatenate([dx[:, k * 8 + q, :] for q in range(8)], axis=1)
        b = jnp.concatenate([bs[:, k * 8 + q, :] for q in range(8)], axis=1)
        cross = jnp.sum(g * b, axis=0, keepdims=True) * (1.0 / 128)
        c_hi, c_lo = split2(cross)
        g_hi, g_lo = split2(g)
        tail = jnp.concatenate(
            [c_hi.astype(F32), c_lo.astype(F32), jnp.zeros((6, 1024), F32)], axis=0
        ).astype(BF16)
        lhs = jnp.concatenate([g_hi, g_hi, g_lo, tail], axis=0)
        both = tn(lhs, rhs)
        normed = xn[pl.ds(base, 1024), :]
        back = rst[pl.ds(base, 1024), :] * (both[:, 0:128] - normed * both[:, 128:256])
        pg[pl.ds(k * 8, 8)] = back.astype(BF16).reshape(8, 128, 128)
        store(k).start()
        n_hi, n_lo = split2(normed)
        g2 = jnp.concatenate([g_hi, g_lo], axis=0)
        part = nn(g2, n_hi) + nn(g2, n_lo)
        pwacc[...] += part[0:8] + part[8:16]

    def sums(k):
        for d in range(1, 4):
            c_oy(k, d).wait_recv()
        rb[k, 0:2] = (
            (oa[k, y].astype(F32) + ra[k, 1].astype(F32))
            + (ra[k, 2].astype(F32) + ra[k, 3].astype(F32))
        ).astype(BF16)
        c_ox(k).wait_recv()
        rb[k, 2:4] = (
            okv[k, c, xh].astype(F32) + rsb[k, xh].astype(F32) + rx[k].astype(F32)
        ).astype(BF16)

    def loop_sum(k, _):
        sums(k)
        c_ra(k).start()
        c_rk(k).start()
        pair_back(k)
        return 0

    lax.fori_loop(1, 8, loop_sum, 0)
    sums(0)
    ret[s] = rb[0]
    pair_back(0)

    def wait_ret(k, _):
        c_ra(k).wait_recv()
        c_rk(k).wait_recv()
        return 0

    lax.fori_loop(1, 8, wait_ret, 0)

    def unshuffle(t, q):
        return jnp.concatenate(
            [ret[h, t][:, q * 32:(q + 1) * 32] for h in range(8)], axis=-1
        )

    for q in range(8):
        rows = pl.ds(q * 64, 64)
        att = unshuffle(0, q).astype(F32)
        open_ = gate[rows, :]
        out = (open_ * att).astype(BF16)
        heads4[0, q] = out
        upd[q] = nn(out, ow[...]).astype(BF16)
        dpj[3, rows, :] = (gg[rows, :] * att * open_ * (1.0 - open_)).astype(BF16)
        for t in range(3):
            dpj[t, rows, :] = unshuffle(t + 1, q)
    for g in range(4):
        w = nn(nbt[...], dpj[g]).reshape(2, 8, 16, 256)
        ch[:, :, g * 16:(g + 1) * 16, :] = w
    w = tn(heads4[0].reshape(512, 256), ug[...].reshape(512, 256)).reshape(2, 8, 16, 256)
    ch[:, :, 64:80, :] = w

    ch[:, :, 80:96, :] = jnp.zeros((2, 8, 16, 256), F32)
    ch[0, 0, 80:88, 0:128] = pwacc[...]

    c_tc().start()
    c_tc().wait_recv()
    ch2[...] = (ch[c] + chr_[...]).astype(BF16)

    def start_ts(k, _):
        c_ts(k).start()
        return 0

    lax.fori_loop(1, 8, start_ts, 0)
    for q in range(8):
        rows = pl.ds(q * 64, 64)
        d = nt(dpj[0, rows, :], cw[:, 0:256])
        for g in range(1, 4):
            d += nt(dpj[g, rows, :], cw[:, g * 256:(g + 1) * 256])
        n = nf[rows, :]
        spread = spb[rows, 0:1]
        mean_d = jnp.mean(d, axis=-1, keepdims=True)
        mean_x = jnp.mean(d * n, axis=-1, keepdims=True)
        alg[q] = (spread * (d - mean_d - n * mean_x)).astype(BF16)
    acc = ch2[s].astype(F32)
    for k in range(1, 8):
        c_ts(k).wait_recv()
        acc += chs[k].astype(F32)
    chx[...] = acc.astype(BF16)
    chy[xh * 4 + y] = chx[...]

    def start_xy(m, _):
        c_txy(m).start()
        return 0

    lax.fori_loop(1, 8, start_xy, 0)
    for m in range(1, 8):
        c_txy(m).wait_recv()
    acc = chy[0].astype(F32)
    for a in range(1, 8):
        acc += chy[a].astype(F32)
    chf[c, s] = acc.astype(BF16)

    def start_as(k, _):
        c_as(k).start()
        return 0

    lax.fori_loop(1, 8, start_as, 0)
    for k in range(1, 8):
        c_as(k).wait_recv()
    c_ac().start()
    c_ac().wait_recv()

    def drain(k, _):
        c_in_qa(k).wait_send()
        c_in_kv(k).wait_send()
        c_pa(k).wait_send()
        c_ra(k).wait_send()
        c_rk(k).wait_send()
        c_da(k).wait_send()
        c_ts(k).wait_send()
        c_as(k).wait_send()
        c_txy(k).wait_send()
        return 0

    lax.fori_loop(1, 8, drain, 0)
    for k in range(8):
        store(k).wait()

    def drain_all(k, _):
        for d in range(1, 4):
            c_gy(k, d).wait_send()
            c_oy(k, d).wait_send()
        c_gx(k).wait_send()
        c_gs(k).wait_send()
        c_gf(k).wait_send()
        c_os(k).wait_send()
        c_ox(k).wait_send()
        return 0

    lax.fori_loop(0, 8, drain_all, 0)
    for d in range(1, 4):
        c_py(d).wait_send()
        c_st(d).wait_send()
        c_dy(d).wait_send()
    c_tc().wait_send()
    c_ac().wait_send()


def finish(upd_in, alg_in, pg_in, chf, upd, alg, pg, dcw, dow, dpw, tok, pair, isem, osem):
    moves = [(pg_in.at[pl.ds(16 * a, 16)], pair.at[a], pg.at[pl.ds(16 * a, 16)]) for a in range(4)]
    moves.append((upd_in, tok.at[0], upd))
    moves.append((alg_in, tok.at[1], alg))
    reads = [pltpu.make_async_copy(m[0], m[1], isem.at[i]) for i, m in enumerate(moves)]
    writes = [pltpu.make_async_copy(m[1], m[2], osem.at[i]) for i, m in enumerate(moves)]
    for copy in reads:
        copy.start()
    for b in range(2):
        for q in range(8):
            at = (b * 8 + q) * 16
            for g in range(4):
                dcw[at:at + 16, g * 256:(g + 1) * 256] = chf[b, q, g * 16:(g + 1) * 16, :].astype(F32)
            dow[at:at + 16, :] = chf[b, q, 64:80, :].astype(F32)
    dpw[...] = chf[0, 0, 80:96, 0:128].astype(F32)[0:8]
    for read, write in zip(reads, writes):
        read.wait()
        write.start()
    for copy in writes:
        copy.wait()


def body(alignment_rows, pair_entries, combined_weight, output_weight, pair_weight, updated_gradient):
    V = pltpu.VMEM
    scratch = [
        V((512, 256), F32),
        V((512, 128), F32),
        V((512, 256), BF16),
        V((256, 512), BF16),
        V((512, 256), F32),
        V((512, 256), F32),
        V((4, 8, 64, 256), BF16),
        V((8, 4, 64, 256), BF16),
        V((8, 4, 2, 64, 256), BF16),
        V((8, 4, 2, 64, 256), BF16),
        V((8192, 128), F32),
        V((8192, 128), F32),
        V((8, 64, 128), F32),
        V((2, 4, 64, 128), F32),
        V((4, 2, 64, 128), F32),
        V((4, 256, 256), BF16),
        V((4, 8, 256), F32),
        V((256, 256), F32),
        V((256, 256), F32),
        V((8, 4, 2, 64, 256), BF16),
        V((8, 2, 2, 2, 64, 256), BF16),
        V((8, 4, 2, 64, 256), BF16),
        V((8, 2, 2, 64, 256), BF16),
        V((8, 2, 64, 256), BF16),
        V((8, 2, 64, 256), BF16),
        V((8, 4, 64, 256), BF16),
        V((8, 4, 64, 256), BF16),
        V((4, 2, 64, 128), F32),
        V((2, 4, 64, 128), F32),
        V((8, 64, 128), F32),
        V((4, 512, 256), BF16),
        V((2, 8, 96, 256), F32),
        V((8, 96, 256), F32),
        V((8, 96, 256), BF16),
        V((8, 96, 256), BF16),
        V((96, 256), BF16),
        V((8, 96, 256), BF16),
        V((8, 128), F32),
        V((64, 128, 128), BF16),
        V((64, 128, 128), BF16),
        pltpu.SemaphoreType.DMA((SEM_COUNT,)),
        pltpu.SemaphoreType.DMA((SEM_COUNT,)),
        pltpu.SemaphoreType.DMA((9,)),
    ]
    vm = pl.BlockSpec(memory_space=pltpu.VMEM)
    hbm = pl.BlockSpec(memory_space=pl.ANY)
    tokens = jax.ShapeDtypeStruct((8, 64, 256), BF16)
    pairs = jax.ShapeDtypeStruct((64, 128, 128), BF16)
    upd, alg, pg, chf = pl.pallas_call(
        kernel,
        out_shape=(tokens, tokens, pairs, jax.ShapeDtypeStruct((2, 8, 96, 256), BF16)),
        in_specs=[vm, hbm, vm, vm, vm, vm],
        out_specs=(vm, vm, hbm, vm),
        scratch_shapes=scratch,
        compiler_params=pltpu.CompilerParams(
            collective_id=0, has_side_effects=True, vmem_limit_bytes=60 << 20
        ),
        name="row_attention",
    )(alignment_rows, pair_entries, combined_weight, output_weight, pair_weight.T, updated_gradient)
    done = pl.pallas_call(
        finish,
        out_shape=(
            tokens,
            tokens,
            pairs,
            jax.ShapeDtypeStruct((256, 1024), F32),
            jax.ShapeDtypeStruct((256, 256), F32),
            jax.ShapeDtypeStruct((8, 128), F32),
        ),
        in_specs=[hbm, hbm, hbm, vm],
        out_specs=(hbm, hbm, hbm, vm, vm, vm),
        scratch_shapes=[
            V((2, 8, 64, 256), BF16),
            V((4, 16, 128, 128), BF16),
            pltpu.SemaphoreType.DMA((6,)),
            pltpu.SemaphoreType.DMA((6,)),
        ],
        compiler_params=pltpu.CompilerParams(vmem_limit_bytes=60 << 20),
        name="results",
    )(upd, alg, pg, chf)
    return *done[:5], done[5].T


def solution(mesh):
    return jax.shard_map(
        body,
        mesh=mesh,
        in_specs=(
            P("seq", "res", None),
            P("res", "seq", None),
            P(),
            P(),
            P(),
            P("seq", "res", None),
        ),
        out_specs=(
            P("seq", "res", None),
            P("seq", "res", None),
            P("res", "seq", None),
            P(),
            P(),
            P(),
        ),
        check_vma=False,
    )
```

```python
import math

import jax
import jax.numpy as jnp
from jax import lax
from jax.experimental import pallas as pl
from jax.experimental.pallas import tpu as pltpu
from jax.sharding import PartitionSpec as P

MESH = pl.DeviceIdType.MESH
EPS = 1e-05
SCALE = 1.0 / math.sqrt(2048)
F32 = jnp.float32
BF16 = jnp.bfloat16

IN_QA, IN_KV, GY, GX, GS, GF = 0, 8, 16, 48, 56, 64
PB_A, PB_Y, STAT = 72, 80, 84
OY, OS, OX, RT_A, RT_K = 88, 120, 128, 136, 144
DL_Y, DL_A = 152, 156
T_C, T_S, T_XY, T_AS, T_AC = 164, 165, 173, 181, 189
SEM_COUNT = 190
LAG = 2


def nt(a, b):
    return lax.dot_general(a, b, (((1,), (1,)), ((), ())), preferred_element_type=F32)


def tn(a, b):
    return lax.dot_general(a, b, (((0,), (0,)), ((), ())), preferred_element_type=F32)


def nn(a, b):
    return jnp.dot(a, b, preferred_element_type=F32)


def split2(v):
    hi = v.astype(BF16)
    lo = (v - hi.astype(F32)).astype(BF16)
    return hi, lo


def split3(v):
    hi = v.astype(BF16)
    rest = v - hi.astype(F32)
    mid = rest.astype(BF16)
    lo = (rest - mid.astype(F32)).astype(BF16)
    return hi, mid, lo


def kernel(
    al_in, pe_in, cw_in, ow_in, pw_in, ug_in,
    upd_out, alg_out, pg_out, chf_out,
    nf, spb, nb, nbt, gate, gg, heads4, sb, qa, kv,
    xn, rst, bs, pb, bi, bt, st, lt, dpt, oa, okv, ra, rsb, xb, rx, rb, ret,
    dl, dr, dx, dpj, ch, chr_, ch2, chs, chx, chy, pwacc,
    al, pe, cw, ow, pw, ug, upd, alg, pg, chf, ssem, rsem, lsem,
):
    s = lax.axis_index("seq")
    r = lax.axis_index("res")
    z, xl = s // 2, s % 2
    xh, y, c = r // 8, (r // 2) % 4, r % 2
    p = xh * 2 + c

    def at_seq(k):
        return {"seq": ((z + k // 2) % 4) * 2 + (xl + k) % 2}

    def from_seq(k):
        return {"seq": ((z + 4 - k // 2) % 4) * 2 + (xl + k) % 2}

    def at_y(d):
        return {"res": xh * 8 + ((y + d) % 4) * 2 + c}

    def at_xy(m):
        return {"res": ((xh + m // 4) % 2) * 8 + ((y + m) % 4) * 2 + c}

    at_x = {"res": (1 - xh) * 8 + y * 2 + c}
    at_c = {"res": xh * 8 + y * 2 + (1 - c)}

    def send(src, dst, i, where):
        return pltpu.make_async_remote_copy(
            src_ref=src, dst_ref=dst, send_sem=ssem.at[i], recv_sem=rsem.at[i],
            device_id=where, device_id_type=MESH,
        )

    loads = [
        pltpu.make_async_copy(a, b, lsem.at[8 + i])
        for i, (a, b) in enumerate(
            ((al_in, al), (cw_in, cw), (ug_in, ug), (ow_in, ow), (pw_in, pw), (pe_in, pe))
        )
    ]
    for load in loads:
        load.start()

    bar = pltpu.get_barrier_semaphore()
    for k in range(1, 8):
        pl.semaphore_signal(bar, inc=1, device_id=at_seq(k), device_id_type=MESH)
        pl.semaphore_signal(bar, inc=1, device_id=at_xy(k), device_id_type=MESH)
    pl.semaphore_signal(bar, inc=1, device_id=at_c, device_id_type=MESH)

    def c_in_qa(k):
        return send(sb.at[at_seq(k)["seq"], pl.ds(0, 2)], qa.at[k, y], IN_QA + k, at_seq(k))

    def c_in_kv(k):
        return send(sb.at[at_seq(k)["seq"], pl.ds(2, 2)], kv.at[k, p], IN_KV + k, at_seq(k))

    def c_gy(k, d):
        return send(qa.at[k, y], qa.at[k, y], GY + k * 4 + d, at_y(d))

    def c_gr(k, d):
        t = 0 if d == 1 else 1
        src = qa.at[k, (y + 4 - d) % 4, t]
        return send(src, src, GY + k * 4 + (0 if d == 1 else 2), at_y(d))

    def c_gx(k):
        return send(kv.at[k, p], kv.at[k, p], GX + k, at_x)

    def c_gs(k):
        return send(kv.at[k, p], kv.at[k, p], GS + k, at_c)

    px = (1 - xh) * 2 + c

    def c_gf(k):
        return send(kv.at[k, px], kv.at[k, px], GF + k, at_c)

    def c_pa(k):
        return send(bs.at[at_seq(k)["seq"]], pb.at[s // 4, s % 4], PB_A + k, at_seq(k))

    def c_py(d):
        return send(pb.at[:, (y + d) % 4], bi.at[y], PB_Y + d, at_y(d))

    def c_st(d):
        return send(st.at[y], st.at[y], STAT + d, at_y(d))

    def c_or(k, d):
        t = 0 if d == 1 else 1
        return send(
            oa.at[k, (y + 2) % 4, t], ra.at[k, 0 if d == 1 else 2, 0],
            OY + k * 4 + (0 if d == 1 else 2), at_y(d),
        )

    def c_oy(k, d):
        return send(oa.at[k, (y + d) % 4], ra.at[k, d], OY + k * 4 + d, at_y(d))

    def c_os(k):
        return send(okv.at[k, 1 - c], rsb.at[k], OS + k, at_c)

    def c_ox(k):
        return send(xb.at[k], rx.at[k], OX + k, at_x)

    def c_ra(k):
        return send(rb.at[k, pl.ds(0, 2)], ret.at[s, pl.ds(0, 2)], RT_A + k, from_seq(k))

    def c_rk(k):
        return send(rb.at[k, pl.ds(2, 2)], ret.at[s, pl.ds(2, 2)], RT_K + k, from_seq(k))

    def c_dy(d):
        return send(dl.at[(y + d) % 4], dr.at[:, y], DL_Y + d, at_y(d))

    def c_da(k):
        w = at_seq(k)["seq"]
        return send(dr.at[w // 4, w % 4], dx.at[s], DL_A + k, at_seq(k))

    def c_tc():
        return send(ch.at[1 - c], chr_, T_C, at_c)

    def c_ts(k):
        return send(ch2.at[at_seq(k)["seq"]], chs.at[k], T_S + k, at_seq(k))

    def c_txy(m):
        return send(chx, chy.at[xh * 4 + y], T_XY + m, at_xy(m))

    def c_as(k):
        return send(chf.at[c, s], chf.at[c, s], T_AS + k, at_seq(k))

    def c_ac():
        return send(chf.at[c], chf.at[c], T_AC, at_c)

    loads[0].wait()
    for q in range(8):
        x = al[q].astype(F32)
        cen = x - jnp.mean(x, axis=-1, keepdims=True)
        spread = lax.rsqrt(jnp.mean(cen * cen, axis=-1, keepdims=True) + EPS)
        normed = cen * spread
        rows = pl.ds(q * 64, 64)
        nf[rows, :] = normed
        spb[rows, :] = jnp.broadcast_to(spread, (64, 128))
        nb[rows, :] = normed.astype(BF16)
    def shuffle(t):
        for h in range(8):
            sb[h, t] = jnp.concatenate(
                [heads4[t, q][:, h * 32:(h + 1) * 32] for q in range(8)], axis=-1
            )

    for load in loads[1:4]:
        load.wait()
    for q in range(8):
        rows = pl.ds(q * 64, 64)
        n = nb[rows, :]
        heads4[0, q] = (nn(n, cw[:, 0:256]) * SCALE).astype(BF16)
        heads4[2, q] = nn(n, cw[:, 256:512]).astype(BF16)
        heads4[3, q] = nn(n, cw[:, 512:768]).astype(BF16)
        open_ = 1.0 / (1.0 + jnp.exp(-nn(n, cw[:, 768:1024])))
        gate[rows, :] = open_
        grad = nt(ug[q], ow[...])
        gg[rows, :] = grad
        heads4[1, q] = (grad * open_).astype(BF16)
    for h in range(8):
        for t in range(4):
            sb[h, t] = jnp.concatenate(
                [heads4[t, q][:, h * 32:(h + 1) * 32] for q in range(8)], axis=-1
            )
    pl.semaphore_wait(bar, 15)

    def start_in(k, _):
        c_in_qa(k).start()
        c_in_kv(k).start()
        return 0

    lax.fori_loop(1, 8, start_in, 0)
    qa[0, y] = sb[s, 0:2]
    kv[0, p] = sb[s, 2:4]
    c_gx(0).start()
    c_gs(0).start()
    for d in (1, 3):
        c_gy(0, d).start()

    for load in loads[4:]:
        load.wait()
    ones = jnp.ones((128, 128), BF16)
    w_all = pw[...]
    w3 = jnp.concatenate(split3(w_all), axis=0)

    def pair_chunk(k):
        base = pl.multiple_of(k * 1024, 1024)
        x = pe[pl.ds(k * 8, 8)].reshape(1024, 128)
        cen = x.astype(F32) - nn(x, ones) * (1.0 / 128)
        hi, lo = split2(cen * cen)
        spread = lax.rsqrt((nn(hi, ones) + nn(lo, ones)) * (1.0 / 128) + EPS)
        normed = cen * spread
        xn[pl.ds(base, 1024), :] = normed
        rst[pl.ds(base, 1024), :] = spread
        hi, lo = split2(normed)
        b = nt(w3, hi) + nt(w3, lo)
        b = b[0:8] + b[8:16] + b[16:24]
        for q in range(8):
            bs[:, k * 8 + q, :] = b[:, q * 128:(q + 1) * 128]

    def stage_in(k, _):
        c_in_qa(k).wait_recv()
        for d in (1, 3):
            c_gy(k, d).start()
        c_in_kv(k).wait_recv()
        c_gx(k).start()
        c_gs(k).start()
        pair_chunk(k)
        return 0

    lax.fori_loop(1, 8, stage_in, 0)
    pair_chunk(0)

    def start_pair(k, _):
        c_pa(k).start()
        return 0

    lax.fori_loop(1, 8, start_pair, 0)
    pb[s // 4, s % 4] = bs[s]

    def share_x(k, _):
        for d in (1, 3):
            c_gy(k, d).wait_recv()
            c_gr(k, d).start()
        c_gx(k).wait_recv()
        c_gf(k).start()
        return 0

    lax.fori_loop(0, 8, share_x, 0)
    nbt[...] = nb[...].T

    def wait_pair(k, _):
        c_pa(k).wait_recv()
        return 0

    lax.fori_loop(1, 8, wait_pair, 0)
    for d in range(1, 4):
        c_py(d).start()
    bi[y] = pb[:, y]

    dpt[...] = jnp.zeros_like(dpt)
    for d in range(1, 4):
        c_py(d).wait_recv()
    bias = jnp.concatenate(
        [jnp.concatenate([bi[a, b] for a in range(4)], axis=0) for b in range(2)], axis=1
    )
    lt[...] = bias.T

    def stage_mm(k, _):
        for d in (1, 3):
            c_gr(k, d).wait_recv()
        c_gs(k).wait_recv()
        c_gf(k).wait_recv()
        qk = qa[k, :, 0].reshape(256, 256)
        dak = qa[k, :, 1].reshape(256, 256)
        kk = kv[k, :, 0].reshape(256, 256)
        vk = kv[k, :, 1].reshape(256, 256)
        lt[...] += nt(kk, qk)
        dpt[...] += nt(vk, dak)
        return 0

    lax.fori_loop(0, 8, stage_mm, 0)
    logits = lt[...]
    top = jnp.max(logits, axis=0, keepdims=True)
    e = jnp.exp(logits - top)
    dp = dpt[...]
    total = jnp.sum(e, axis=0, keepdims=True)
    dots = jnp.sum(e * dp, axis=0, keepdims=True)
    st[y] = jnp.concatenate([top, total, dots, jnp.zeros((5, 256), F32)], axis=0)
    for d in range(1, 4):
        c_st(d).start()
    lt[...] = e
    for d in range(1, 4):
        c_st(d).wait_recv()
    stats = [st[a] for a in range(4)]
    peak = jnp.maximum(
        jnp.maximum(stats[0][0:1], stats[1][0:1]), jnp.maximum(stats[2][0:1], stats[3][0:1])
    )
    z_sum = jnp.zeros((1, 256), F32)
    d_sum = jnp.zeros((1, 256), F32)
    for a in range(4):
        f = jnp.exp(stats[a][0:1] - peak)
        z_sum += f * stats[a][1:2]
        d_sum += f * stats[a][2:3]
    inv = 1.0 / z_sum
    mine = st[y]
    prob_t = lt[...] * (jnp.exp(mine[0:1] - peak) * inv)
    grad_t = prob_t * (dpt[...] - d_sum * inv)
    lt[...] = prob_t
    dpt[...] = grad_t
    grad = grad_t.T
    for a in range(4):
        for b in range(2):
            dl[a, b] = grad[a * 64:(a + 1) * 64, b * 128:(b + 1) * 128]
    for d in range(1, 4):
        c_dy(d).start()
    dr[:, y] = dl[y]
    bt[0] = lt[...].astype(BF16)
    bt[1] = bt[0].T
    bt[2] = dpt[...].astype(BF16)
    bt[3] = grad.astype(BF16)

    def stage_out(k):
        qk = qa[k, :, 0].reshape(256, 256)
        dak = qa[k, :, 1].reshape(256, 256)
        kk = kv[k, :, 0].reshape(256, 256)
        vk = kv[k, :, 1].reshape(256, 256)
        oa[k, :, 0] = nn(bt[1], vk).astype(BF16).reshape(4, 64, 256)
        oa[k, :, 1] = (nn(bt[3], kk) * SCALE).astype(BF16).reshape(4, 64, 256)
        for d in (1, 3):
            c_or(k, d).start()
        dk = nn(bt[2], qk).astype(BF16)
        dv = nn(bt[0], dak).astype(BF16)
        for a in range(2):
            for b in range(2):
                at = (a * 2 + b) * 64
                okv[k, b, a, 0] = dk[at:at + 64]
                okv[k, b, a, 1] = dv[at:at + 64]
        c_os(k).start()

    def stage_y(k):
        for d in (1, 3):
            t = 0 if d == 1 else 1
            c_or(k, d).wait_recv()
            to = (y + d) % 4
            oa[k, to, t] = (
                oa[k, to, t].astype(F32) + ra[k, 0 if d == 1 else 2, 0].astype(F32)
            ).astype(BF16)
            c_oy(k, d).start()

    def stage_x(k):
        c_os(k).wait_recv()
        xb[k] = (okv[k, c, 1 - xh].astype(F32) + rsb[k, 1 - xh].astype(F32)).astype(BF16)
        c_ox(k).start()

    stage_out(1)

    def loop_out(i, _):
        stage_out((i + 1) % 8)
        stage_x(i)

        @pl.when(i > LAG)
        def _relay():
            stage_y(i - LAG)

        return 0

    lax.fori_loop(1, 8, loop_out, 0)
    stage_x(0)
    for i in range(8 - LAG, 9):
        stage_y(i % 8)

    for d in range(1, 4):
        c_dy(d).wait_recv()

    def start_da(k, _):
        c_da(k).start()
        return 0

    lax.fori_loop(1, 8, start_da, 0)
    dx[s] = dr[s // 4, s % 4]

    def wait_da(k, _):
        c_da(k).wait_recv()
        return 0

    lax.fori_loop(1, 8, wait_da, 0)
    w_mean = jnp.mean(w_all, axis=-1, keepdims=True)
    v_hi, v_mid, _ = split3(w_all - w_mean)
    one_rows = jnp.where(
        lax.broadcasted_iota(jnp.int32, (8, 128), 0) < 2, 1.0, 0.0
    ).astype(BF16)
    zero_rows = jnp.zeros((8, 128), BF16)
    rhs = jnp.concatenate(
        [
            jnp.concatenate([v_hi, zero_rows], axis=1),
            jnp.concatenate([v_mid, zero_rows], axis=1),
            jnp.concatenate([v_hi, zero_rows], axis=1),
            jnp.concatenate([zero_rows, one_rows], axis=1),
        ],
        axis=0,
    )
    pwacc[...] = jnp.zeros_like(pwacc)

    def store(k):
        rows = pl.ds(k * 8, 8)
        return pltpu.make_async_copy(pg.at[rows], pg_out.at[rows], lsem.at[k])

    def pair_back(k, _):
        base = pl.multiple_of(k * 1024, 1024)
        g = jnp.concatenate([dx[:, k * 8 + q, :] for q in range(8)], axis=1)
        b = jnp.concatenate([bs[:, k * 8 + q, :] for q in range(8)], axis=1)
        cross = jnp.sum(g * b, axis=0, keepdims=True) * (1.0 / 128)
        c_hi, c_lo = split2(cross)
        g_hi, g_lo = split2(g)
        tail = jnp.concatenate(
            [c_hi.astype(F32), c_lo.astype(F32), jnp.zeros((6, 1024), F32)], axis=0
        ).astype(BF16)
        lhs = jnp.concatenate([g_hi, g_hi, g_lo, tail], axis=0)
        both = tn(lhs, rhs)
        normed = xn[pl.ds(base, 1024), :]
        back = rst[pl.ds(base, 1024), :] * (both[:, 0:128] - normed * both[:, 128:256])
        pg[pl.ds(k * 8, 8)] = back.astype(BF16).reshape(8, 128, 128)
        store(k).start()
        n_hi, n_lo = split2(normed)
        g2 = jnp.concatenate([g_hi, g_lo], axis=0)
        part = nn(g2, n_hi) + nn(g2, n_lo)
        pwacc[...] += part[0:8] + part[8:16]
        return 0

    def sums(k):
        for d in (1, 3):
            c_oy(k, d).wait_recv()
        rb[k, 0:2] = (
            oa[k, y].astype(F32) + (ra[k, 1].astype(F32) + ra[k, 3].astype(F32))
        ).astype(BF16)
        c_ox(k).wait_recv()
        rb[k, 2:4] = (
            okv[k, c, xh].astype(F32) + rsb[k, xh].astype(F32) + rx[k].astype(F32)
        ).astype(BF16)

    def loop_sum(k, _):
        sums(k)
        c_ra(k).start()
        c_rk(k).start()
        return 0

    lax.fori_loop(1, 8, loop_sum, 0)
    sums(0)
    ret[s] = rb[0]
    lax.fori_loop(0, 8, pair_back, 0)

    def drain_in(k, _):
        c_in_qa(k).wait_send()
        c_in_kv(k).wait_send()
        c_pa(k).wait_send()
        return 0

    lax.fori_loop(1, 8, drain_in, 0)

    def drain_gather(k, _):
        for d in (1, 3):
            c_gy(k, d).wait_send()
            c_gr(k, d).wait_send()
        c_gx(k).wait_send()
        c_gs(k).wait_send()
        c_gf(k).wait_send()
        return 0

    lax.fori_loop(0, 8, drain_gather, 0)

    def wait_ret(k, _):
        c_ra(k).wait_recv()
        c_rk(k).wait_recv()
        return 0

    lax.fori_loop(1, 8, wait_ret, 0)

    def unshuffle(t, q):
        return jnp.concatenate(
            [ret[h, t][:, q * 32:(q + 1) * 32] for h in range(8)], axis=-1
        )

    for q in range(8):
        rows = pl.ds(q * 64, 64)
        att = unshuffle(0, q).astype(F32)
        open_ = gate[rows, :]
        out = (open_ * att).astype(BF16)
        heads4[0, q] = out
        upd[q] = nn(out, ow[...]).astype(BF16)
        dpj[3, rows, :] = (gg[rows, :] * att * open_ * (1.0 - open_)).astype(BF16)
        for t in range(3):
            dpj[t, rows, :] = unshuffle(t + 1, q)
    put_upd = pltpu.make_async_copy(upd, upd_out, lsem.at[14])
    put_upd.start()
    for g in range(4):
        w = nn(nbt[...], dpj[g]).reshape(2, 8, 16, 256)
        ch[:, :, g * 16:(g + 1) * 16, :] = w
    w = tn(heads4[0].reshape(512, 256), ug[...].reshape(512, 256)).reshape(2, 8, 16, 256)
    ch[:, :, 64:80, :] = w

    ch[:, :, 80:96, :] = jnp.zeros((2, 8, 16, 256), F32)
    ch[0, 0, 80:88, 0:128] = pwacc[...]

    c_tc().start()
    c_tc().wait_recv()
    ch2[...] = (ch[c] + chr_[...]).astype(BF16)

    def start_ts(k, _):
        c_ts(k).start()
        return 0

    lax.fori_loop(1, 8, start_ts, 0)
    for q in range(8):
        rows = pl.ds(q * 64, 64)
        d = nt(dpj[0, rows, :], cw[:, 0:256])
        for g in range(1, 4):
            d += nt(dpj[g, rows, :], cw[:, g * 256:(g + 1) * 256])
        n = nf[rows, :]
        spread = spb[rows, 0:1]
        mean_d = jnp.mean(d, axis=-1, keepdims=True)
        mean_x = jnp.mean(d * n, axis=-1, keepdims=True)
        alg[q] = (spread * (d - mean_d - n * mean_x)).astype(BF16)
    put_alg = pltpu.make_async_copy(alg, alg_out, lsem.at[15])
    put_alg.start()

    def drain_out(k, _):
        for d in (1, 3):
            c_or(k, d).wait_send()
            c_oy(k, d).wait_send()
        c_os(k).wait_send()
        c_ox(k).wait_send()
        return 0

    lax.fori_loop(0, 8, drain_out, 0)

    def drain_ret(k, _):
        c_ra(k).wait_send()
        c_rk(k).wait_send()
        c_da(k).wait_send()
        return 0

    lax.fori_loop(1, 8, drain_ret, 0)
    for d in range(1, 4):
        c_py(d).wait_send()
        c_st(d).wait_send()
        c_dy(d).wait_send()
    for k in range(8):
        store(k).wait()
    put_upd.wait()
    put_alg.wait()
    acc = ch2[s].astype(F32)
    for k in range(1, 8):
        c_ts(k).wait_recv()
        acc += chs[k].astype(F32)
    chx[...] = acc.astype(BF16)
    chy[xh * 4 + y] = chx[...]

    def start_xy(m, _):
        c_txy(m).start()
        return 0

    lax.fori_loop(1, 8, start_xy, 0)
    for m in range(1, 8):
        c_txy(m).wait_recv()
    acc = chy[0].astype(F32)
    for a in range(1, 8):
        acc += chy[a].astype(F32)
    chf[c, s] = acc.astype(BF16)

    def start_as(k, _):
        c_as(k).start()
        return 0

    lax.fori_loop(1, 8, start_as, 0)
    for k in range(1, 8):
        c_as(k).wait_recv()
    c_ac().start()
    c_ac().wait_recv()

    put_sum = pltpu.make_async_copy(chf, chf_out, lsem.at[16])
    put_sum.start()

    def drain(k, _):
        c_ts(k).wait_send()
        c_as(k).wait_send()
        c_txy(k).wait_send()
        return 0

    lax.fori_loop(1, 8, drain, 0)
    c_tc().wait_send()
    c_ac().wait_send()
    put_sum.wait()


def finish(upd_in, alg_in, pg_in, chf, upd, alg, pg, dcw, dow, dpw, tok, pair, isem, osem):
    moves = [(pg_in.at[pl.ds(16 * a, 16)], pair.at[a], pg.at[pl.ds(16 * a, 16)]) for a in range(4)]
    moves.append((upd_in, tok.at[0], upd))
    moves.append((alg_in, tok.at[1], alg))
    reads = [pltpu.make_async_copy(m[0], m[1], isem.at[i]) for i, m in enumerate(moves)]
    writes = [pltpu.make_async_copy(m[1], m[2], osem.at[i]) for i, m in enumerate(moves)]
    for copy in reads:
        copy.start()
    for b in range(2):
        for q in range(8):
            at = (b * 8 + q) * 16
            for g in range(4):
                dcw[at:at + 16, g * 256:(g + 1) * 256] = chf[b, q, g * 16:(g + 1) * 16, :].astype(F32)
            dow[at:at + 16, :] = chf[b, q, 64:80, :].astype(F32)
    dpw[...] = chf[0, 0, 80:96, 0:128].astype(F32)[0:8]
    for read, write in zip(reads, writes):
        read.wait()
        write.start()
    for copy in writes:
        copy.wait()


def body(alignment_rows, pair_entries, combined_weight, output_weight, pair_weight, updated_gradient):
    V = pltpu.VMEM
    scratch = [
        V((512, 256), F32),
        V((512, 128), F32),
        V((512, 256), BF16),
        V((256, 512), BF16),
        V((512, 256), F32),
        V((512, 256), F32),
        V((4, 8, 64, 256), BF16),
        V((8, 4, 64, 256), BF16),
        V((8, 4, 2, 64, 256), BF16),
        V((8, 4, 2, 64, 256), BF16),
        V((8192, 128), F32),
        V((8192, 128), F32),
        V((8, 64, 128), F32),
        V((2, 4, 64, 128), F32),
        V((4, 2, 64, 128), F32),
        V((4, 256, 256), BF16),
        V((4, 8, 256), F32),
        V((256, 256), F32),
        V((256, 256), F32),
        V((8, 4, 2, 64, 256), BF16),
        V((8, 2, 2, 2, 64, 256), BF16),
        V((8, 4, 2, 64, 256), BF16),
        V((8, 2, 2, 64, 256), BF16),
        V((8, 2, 64, 256), BF16),
        V((8, 2, 64, 256), BF16),
        V((8, 4, 64, 256), BF16),
        V((8, 4, 64, 256), BF16),
        V((4, 2, 64, 128), F32),
        V((2, 4, 64, 128), F32),
        V((8, 64, 128), F32),
        V((4, 512, 256), BF16),
        V((2, 8, 96, 256), F32),
        V((8, 96, 256), F32),
        V((8, 96, 256), BF16),
        V((8, 96, 256), BF16),
        V((96, 256), BF16),
        V((8, 96, 256), BF16),
        V((8, 128), F32),
        V((8, 64, 256), BF16),
        V((64, 128, 128), BF16),
        V((256, 1024), BF16),
        V((256, 256), BF16),
        V((8, 128), F32),
        V((8, 64, 256), BF16),
        V((8, 64, 256), BF16),
        V((8, 64, 256), BF16),
        V((64, 128, 128), BF16),
        V((2, 8, 96, 256), BF16),
        pltpu.SemaphoreType.DMA((SEM_COUNT,)),
        pltpu.SemaphoreType.DMA((SEM_COUNT,)),
        pltpu.SemaphoreType.DMA((17,)),
    ]
    vm = pl.BlockSpec(memory_space=pltpu.VMEM)
    hbm = pl.BlockSpec(memory_space=pl.ANY)
    tokens = jax.ShapeDtypeStruct((8, 64, 256), BF16)
    pairs = jax.ShapeDtypeStruct((64, 128, 128), BF16)
    upd, alg, pg, chf = pl.pallas_call(
        kernel,
        out_shape=(tokens, tokens, pairs, jax.ShapeDtypeStruct((2, 8, 96, 256), BF16)),
        in_specs=[hbm] * 6,
        out_specs=(hbm,) * 4,
        scratch_shapes=scratch,
        compiler_params=pltpu.CompilerParams(
            collective_id=0, has_side_effects=True, vmem_limit_bytes=60 << 20
        ),
        name="row_attention",
    )(alignment_rows, pair_entries, combined_weight, output_weight, pair_weight.T, updated_gradient)
    done = pl.pallas_call(
        finish,
        out_shape=(
            tokens,
            tokens,
            pairs,
            jax.ShapeDtypeStruct((256, 1024), F32),
            jax.ShapeDtypeStruct((256, 256), F32),
            jax.ShapeDtypeStruct((8, 128), F32),
        ),
        in_specs=[hbm, hbm, hbm, vm],
        out_specs=(hbm, hbm, hbm, vm, vm, vm),
        scratch_shapes=[
            V((2, 8, 64, 256), BF16),
            V((4, 16, 128, 128), BF16),
            pltpu.SemaphoreType.DMA((6,)),
            pltpu.SemaphoreType.DMA((6,)),
        ],
        compiler_params=pltpu.CompilerParams(vmem_limit_bytes=60 << 20),
        name="results",
    )(upd, alg, pg, chf)
    return *done[:5], done[5].T


def solution(mesh):
    return jax.shard_map(
        body,
        mesh=mesh,
        in_specs=(
            P("seq", "res", None),
            P("res", "seq", None),
            P(),
            P(),
            P(),
            P("seq", "res", None),
        ),
        out_specs=(
            P("seq", "res", None),
            P("seq", "res", None),
            P("res", "seq", None),
            P(),
            P(),
            P(),
        ),
        check_vma=False,
    )
```

```python
import math

import jax
import jax.numpy as jnp
from jax import lax
from jax.experimental import pallas as pl
from jax.experimental.pallas import tpu as pltpu
from jax.sharding import PartitionSpec as P

MESH = pl.DeviceIdType.MESH
EPS = 1e-05
SCALE = 1.0 / math.sqrt(2048)
F32 = jnp.float32
BF16 = jnp.bfloat16

IN_QA, IN_KV, GY, GX, GS, GF = 0, 8, 16, 48, 56, 64
PB_A, PB_Y, STAT = 72, 80, 84
OY, OS, OX, RT_A, RT_K = 88, 120, 128, 136, 144
DL_Y, DL_A = 152, 156
T_C, T_S, T_XY, T_AS, T_AC = 164, 165, 173, 181, 189
SEM_COUNT = 190
LAG = 3


def nt(a, b):
    return lax.dot_general(a, b, (((1,), (1,)), ((), ())), preferred_element_type=F32)


def tn(a, b):
    return lax.dot_general(a, b, (((0,), (0,)), ((), ())), preferred_element_type=F32)


def nn(a, b):
    return jnp.dot(a, b, preferred_element_type=F32)


def split2(v):
    hi = v.astype(BF16)
    lo = (v - hi.astype(F32)).astype(BF16)
    return hi, lo


def split3(v):
    hi = v.astype(BF16)
    rest = v - hi.astype(F32)
    mid = rest.astype(BF16)
    lo = (rest - mid.astype(F32)).astype(BF16)
    return hi, mid, lo


def kernel(
    al_in, pe_in, cw_in, ow_in, pw_in, ug_in,
    upd_out, alg_out, pg_out, chf_out,
    nf, spb, nb, nbt, gate, gg, heads4, sb, qa, kv,
    xn, rst, bs, pb, bi, bt, st, lt, dpt, oa, okv, ra, rsb, xb, rx, rb, ret,
    dl, dr, dx, dpj, ch, chr_, ch2, chs, chx, chy, pwacc,
    al, pe, cw, ow, pw, ug, upd, alg, pg, chf, ssem, rsem, lsem,
):
    s = lax.axis_index("seq")
    r = lax.axis_index("res")
    z, xl = s // 2, s % 2
    xh, y, c = r // 8, (r // 2) % 4, r % 2
    p = xh * 2 + c

    def at_seq(k):
        return {"seq": ((z + k // 2) % 4) * 2 + (xl + k) % 2}

    def from_seq(k):
        return {"seq": ((z + 4 - k // 2) % 4) * 2 + (xl + k) % 2}

    def at_y(d):
        return {"res": xh * 8 + ((y + d) % 4) * 2 + c}

    def at_xy(m):
        return {"res": ((xh + m // 4) % 2) * 8 + ((y + m) % 4) * 2 + c}

    at_x = {"res": (1 - xh) * 8 + y * 2 + c}
    at_c = {"res": xh * 8 + y * 2 + (1 - c)}

    def send(src, dst, i, where):
        return pltpu.make_async_remote_copy(
            src_ref=src, dst_ref=dst, send_sem=ssem.at[i], recv_sem=rsem.at[i],
            device_id=where, device_id_type=MESH,
        )

    loads = [
        pltpu.make_async_copy(a, b, lsem.at[8 + i])
        for i, (a, b) in enumerate(
            ((al_in, al), (cw_in, cw), (ug_in, ug), (ow_in, ow), (pw_in, pw), (pe_in, pe))
        )
    ]
    for load in loads:
        load.start()

    bar = pltpu.get_barrier_semaphore()
    for k in range(1, 8):
        pl.semaphore_signal(bar, inc=1, device_id=at_seq(k), device_id_type=MESH)
        pl.semaphore_signal(bar, inc=1, device_id=at_xy(k), device_id_type=MESH)
    pl.semaphore_signal(bar, inc=1, device_id=at_c, device_id_type=MESH)

    def c_in_qa(k):
        return send(sb.at[at_seq(k)["seq"], pl.ds(0, 2)], qa.at[k, y], IN_QA + k, at_seq(k))

    def c_in_kv(k):
        return send(sb.at[at_seq(k)["seq"], pl.ds(2, 2)], kv.at[k, p], IN_KV + k, at_seq(k))

    def c_gy(k, d):
        return send(qa.at[k, y], qa.at[k, y], GY + k * 4 + d, at_y(d))

    def c_gr(k, d):
        t = 0 if d == 1 else 1
        src = qa.at[k, (y + 4 - d) % 4, t]
        return send(src, src, GY + k * 4 + (0 if d == 1 else 2), at_y(d))

    def c_gx(k):
        return send(kv.at[k, p], kv.at[k, p], GX + k, at_x)

    def c_gs(k):
        return send(kv.at[k, p], kv.at[k, p], GS + k, at_c)

    px = (1 - xh) * 2 + c

    def c_gf(k):
        return send(kv.at[k, px], kv.at[k, px], GF + k, at_c)

    def c_pa(k):
        return send(bs.at[at_seq(k)["seq"]], pb.at[s // 4, s % 4], PB_A + k, at_seq(k))

    def c_py(d):
        return send(pb.at[:, (y + d) % 4], bi.at[y], PB_Y + d, at_y(d))

    def c_st(d):
        return send(st.at[y], st.at[y], STAT + d, at_y(d))

    def c_or(k, d):
        t = 0 if d == 1 else 1
        return send(
            oa.at[k, (y + 2) % 4, t], ra.at[k, 0 if d == 1 else 2, 0],
            OY + k * 4 + (0 if d == 1 else 2), at_y(d),
        )

    def c_oy(k, d):
        return send(oa.at[k, (y + d) % 4], ra.at[k, d], OY + k * 4 + d, at_y(d))

    def c_os(k):
        return send(okv.at[k, 1 - c], rsb.at[k], OS + k, at_c)

    def c_ox(k):
        return send(xb.at[k], rx.at[k], OX + k, at_x)

    def c_ra(k):
        return send(rb.at[k, pl.ds(0, 2)], ret.at[s, pl.ds(0, 2)], RT_A + k, from_seq(k))

    def c_rk(k):
        return send(rb.at[k, pl.ds(2, 2)], ret.at[s, pl.ds(2, 2)], RT_K + k, from_seq(k))

    def c_dy(d):
        return send(dl.at[(y + d) % 4], dr.at[:, y], DL_Y + d, at_y(d))

    def c_da(k):
        w = at_seq(k)["seq"]
        return send(dr.at[w // 4, w % 4], dx.at[s], DL_A + k, at_seq(k))

    def c_tc():
        return send(ch.at[1 - c], chr_, T_C, at_c)

    def c_ts(k):
        return send(ch2.at[at_seq(k)["seq"]], chs.at[k], T_S + k, at_seq(k))

    def c_txy(m):
        return send(chx, chy.at[xh * 4 + y], T_XY + m, at_xy(m))

    def c_as(k):
        return send(chf.at[c, s], chf.at[c, s], T_AS + k, at_seq(k))

    def c_ac():
        return send(chf.at[c], chf.at[c], T_AC, at_c)

    loads[0].wait()
    for q in range(8):
        x = al[q].astype(F32)
        cen = x - jnp.mean(x, axis=-1, keepdims=True)
        spread = lax.rsqrt(jnp.mean(cen * cen, axis=-1, keepdims=True) + EPS)
        normed = cen * spread
        rows = pl.ds(q * 64, 64)
        nf[rows, :] = normed
        spb[rows, :] = jnp.broadcast_to(spread, (64, 128))
        nb[rows, :] = normed.astype(BF16)
    def shuffle(t):
        for h in range(8):
            sb[h, t] = jnp.concatenate(
                [heads4[t, q][:, h * 32:(h + 1) * 32] for q in range(8)], axis=-1
            )

    for load in loads[1:4]:
        load.wait()
    for q in range(8):
        rows = pl.ds(q * 64, 64)
        n = nb[rows, :]
        heads4[0, q] = (nn(n, cw[:, 0:256]) * SCALE).astype(BF16)
        heads4[2, q] = nn(n, cw[:, 256:512]).astype(BF16)
        heads4[3, q] = nn(n, cw[:, 512:768]).astype(BF16)
        open_ = 1.0 / (1.0 + jnp.exp(-nn(n, cw[:, 768:1024])))
        gate[rows, :] = open_
        grad = nt(ug[q], ow[...])
        gg[rows, :] = grad
        heads4[1, q] = (grad * open_).astype(BF16)
    for h in range(8):
        for t in range(4):
            sb[h, t] = jnp.concatenate(
                [heads4[t, q][:, h * 32:(h + 1) * 32] for q in range(8)], axis=-1
            )
    pl.semaphore_wait(bar, 15)

    def start_in(k, _):
        c_in_kv(k).start()
        c_in_qa(k).start()
        return 0

    lax.fori_loop(1, 8, start_in, 0)
    qa[0, y] = sb[s, 0:2]
    kv[0, p] = sb[s, 2:4]
    c_gx(0).start()
    c_gs(0).start()
    for d in (1, 3):
        c_gy(0, d).start()

    for load in loads[4:]:
        load.wait()
    ones = jnp.ones((128, 128), BF16)
    w_all = pw[...]
    w3 = jnp.concatenate(split3(w_all), axis=0)

    def pair_chunk(k):
        base = pl.multiple_of(k * 1024, 1024)
        x = pe[pl.ds(k * 8, 8)].reshape(1024, 128)
        cen = x.astype(F32) - nn(x, ones) * (1.0 / 128)
        hi, lo = split2(cen * cen)
        spread = lax.rsqrt((nn(hi, ones) + nn(lo, ones)) * (1.0 / 128) + EPS)
        normed = cen * spread
        xn[pl.ds(base, 1024), :] = normed
        rst[pl.ds(base, 1024), :] = spread
        hi, lo = split2(normed)
        b = nt(w3, hi) + nt(w3, lo)
        b = b[0:8] + b[8:16] + b[16:24]
        for q in range(8):
            bs[:, k * 8 + q, :] = b[:, q * 128:(q + 1) * 128]

    def stage_in(k, _):
        c_in_kv(k).wait_recv()
        c_gx(k).start()
        c_gs(k).start()
        c_in_qa(k).wait_recv()
        for d in (1, 3):
            c_gy(k, d).start()
        pair_chunk(k)
        return 0

    lax.fori_loop(1, 8, stage_in, 0)
    pair_chunk(0)

    def start_pair(k, _):
        c_pa(k).start()
        return 0

    lax.fori_loop(1, 8, start_pair, 0)
    pb[s // 4, s % 4] = bs[s]

    def share_x(k, _):
        for d in (1, 3):
            c_gy(k, d).wait_recv()
            c_gr(k, d).start()
        c_gx(k).wait_recv()
        c_gf(k).start()
        return 0

    lax.fori_loop(0, 8, share_x, 0)
    nbt[...] = nb[...].T

    def wait_pair(k, _):
        c_pa(k).wait_recv()
        return 0

    lax.fori_loop(1, 8, wait_pair, 0)
    for d in range(1, 4):
        c_py(d).start()
    bi[y] = pb[:, y]

    dpt[...] = jnp.zeros_like(dpt)
    for d in range(1, 4):
        c_py(d).wait_recv()
    bias = jnp.concatenate(
        [jnp.concatenate([bi[a, b] for a in range(4)], axis=0) for b in range(2)], axis=1
    )
    lt[...] = bias.T

    def stage_mm(k, _):
        for d in (1, 3):
            c_gr(k, d).wait_recv()
        c_gs(k).wait_recv()
        c_gf(k).wait_recv()
        qk = qa[k, :, 0].reshape(256, 256)
        dak = qa[k, :, 1].reshape(256, 256)
        kk = kv[k, :, 0].reshape(256, 256)
        vk = kv[k, :, 1].reshape(256, 256)
        lt[...] += nt(kk, qk)
        dpt[...] += nt(vk, dak)
        return 0

    lax.fori_loop(0, 8, stage_mm, 0)
    logits = lt[...]
    top = jnp.max(logits, axis=0, keepdims=True)
    e = jnp.exp(logits - top)
    dp = dpt[...]
    total = jnp.sum(e, axis=0, keepdims=True)
    dots = jnp.sum(e * dp, axis=0, keepdims=True)
    st[y] = jnp.concatenate([top, total, dots, jnp.zeros((5, 256), F32)], axis=0)
    for d in range(1, 4):
        c_st(d).start()
    lt[...] = e
    for d in range(1, 4):
        c_st(d).wait_recv()
    stats = [st[a] for a in range(4)]
    peak = jnp.maximum(
        jnp.maximum(stats[0][0:1], stats[1][0:1]), jnp.maximum(stats[2][0:1], stats[3][0:1])
    )
    z_sum = jnp.zeros((1, 256), F32)
    d_sum = jnp.zeros((1, 256), F32)
    for a in range(4):
        f = jnp.exp(stats[a][0:1] - peak)
        z_sum += f * stats[a][1:2]
        d_sum += f * stats[a][2:3]
    inv = 1.0 / z_sum
    mine = st[y]
    prob_t = lt[...] * (jnp.exp(mine[0:1] - peak) * inv)
    grad_t = prob_t * (dpt[...] - d_sum * inv)
    lt[...] = prob_t
    dpt[...] = grad_t
    grad = grad_t.T
    for a in range(4):
        for b in range(2):
            dl[a, b] = grad[a * 64:(a + 1) * 64, b * 128:(b + 1) * 128]
    for d in range(1, 4):
        c_dy(d).start()
    dr[:, y] = dl[y]
    bt[0] = lt[...].astype(BF16)
    bt[1] = bt[0].T
    bt[2] = dpt[...].astype(BF16)
    bt[3] = grad.astype(BF16)

    def stage_out(k):
        qk = qa[k, :, 0].reshape(256, 256)
        dak = qa[k, :, 1].reshape(256, 256)
        kk = kv[k, :, 0].reshape(256, 256)
        vk = kv[k, :, 1].reshape(256, 256)
        oa[k, :, 0] = nn(bt[1], vk).astype(BF16).reshape(4, 64, 256)
        oa[k, :, 1] = (nn(bt[3], kk) * SCALE).astype(BF16).reshape(4, 64, 256)
        for d in (1, 3):
            c_or(k, d).start()
        dk = nn(bt[2], qk).astype(BF16)
        dv = nn(bt[0], dak).astype(BF16)
        for a in range(2):
            for b in range(2):
                at = (a * 2 + b) * 64
                okv[k, b, a, 0] = dk[at:at + 64]
                okv[k, b, a, 1] = dv[at:at + 64]
        c_os(k).start()

    def stage_y(k):
        for d in (1, 3):
            t = 0 if d == 1 else 1
            c_or(k, d).wait_recv()
            to = (y + d) % 4
            oa[k, to, t] = (
                oa[k, to, t].astype(F32) + ra[k, 0 if d == 1 else 2, 0].astype(F32)
            ).astype(BF16)
            c_oy(k, d).start()

    def stage_x(k):
        c_os(k).wait_recv()
        xb[k] = (okv[k, c, 1 - xh].astype(F32) + rsb[k, 1 - xh].astype(F32)).astype(BF16)
        c_ox(k).start()

    stage_out(1)

    def loop_out(i, _):
        stage_out((i + 1) % 8)
        stage_x(i)

        @pl.when(i > LAG)
        def _relay():
            stage_y(i - LAG)

        return 0

    lax.fori_loop(1, 8, loop_out, 0)
    stage_x(0)
    for i in range(8 - LAG, 9):
        stage_y(i % 8)

    for d in range(1, 4):
        c_dy(d).wait_recv()

    def start_da(k, _):
        c_da(k).start()
        return 0

    lax.fori_loop(1, 8, start_da, 0)
    dx[s] = dr[s // 4, s % 4]

    def wait_da(k, _):
        c_da(k).wait_recv()
        return 0

    lax.fori_loop(1, 8, wait_da, 0)
    w_mean = jnp.mean(w_all, axis=-1, keepdims=True)
    v_hi, v_mid, _ = split3(w_all - w_mean)
    one_rows = jnp.where(
        lax.broadcasted_iota(jnp.int32, (8, 128), 0) < 2, 1.0, 0.0
    ).astype(BF16)
    zero_rows = jnp.zeros((8, 128), BF16)
    rhs = jnp.concatenate(
        [
            jnp.concatenate([v_hi, zero_rows], axis=1),
            jnp.concatenate([v_mid, zero_rows], axis=1),
            jnp.concatenate([v_hi, zero_rows], axis=1),
            jnp.concatenate([zero_rows, one_rows], axis=1),
        ],
        axis=0,
    )
    pwacc[...] = jnp.zeros_like(pwacc)

    def store(k):
        rows = pl.ds(k * 8, 8)
        return pltpu.make_async_copy(pg.at[rows], pg_out.at[rows], lsem.at[k])

    def pair_back(k, _):
        base = pl.multiple_of(k * 1024, 1024)
        g = jnp.concatenate([dx[:, k * 8 + q, :] for q in range(8)], axis=1)
        b = jnp.concatenate([bs[:, k * 8 + q, :] for q in range(8)], axis=1)
        cross = jnp.sum(g * b, axis=0, keepdims=True) * (1.0 / 128)
        c_hi, c_lo = split2(cross)
        g_hi, g_lo = split2(g)
        tail = jnp.concatenate(
            [c_hi.astype(F32), c_lo.astype(F32), jnp.zeros((6, 1024), F32)], axis=0
        ).astype(BF16)
        lhs = jnp.concatenate([g_hi, g_hi, g_lo, tail], axis=0)
        both = tn(lhs, rhs)
        normed = xn[pl.ds(base, 1024), :]
        back = rst[pl.ds(base, 1024), :] * (both[:, 0:128] - normed * both[:, 128:256])
        pg[pl.ds(k * 8, 8)] = back.astype(BF16).reshape(8, 128, 128)
        store(k).start()
        n_hi, n_lo = split2(normed)
        g2 = jnp.concatenate([g_hi, g_lo], axis=0)
        part = nn(g2, n_hi) + nn(g2, n_lo)
        pwacc[...] += part[0:8] + part[8:16]
        return 0

    def sums(k):
        for d in (1, 3):
            c_oy(k, d).wait_recv()
        rb[k, 0:2] = (
            oa[k, y].astype(F32) + (ra[k, 1].astype(F32) + ra[k, 3].astype(F32))
        ).astype(BF16)
        c_ox(k).wait_recv()
        rb[k, 2:4] = (
            okv[k, c, xh].astype(F32) + rsb[k, xh].astype(F32) + rx[k].astype(F32)
        ).astype(BF16)

    def loop_sum(k, _):
        sums(k)
        c_ra(k).start()
        c_rk(k).start()
        return 0

    lax.fori_loop(1, 8, loop_sum, 0)
    sums(0)
    ret[s] = rb[0]
    lax.fori_loop(0, 8, pair_back, 0)

    def drain_in(k, _):
        c_in_qa(k).wait_send()
        c_in_kv(k).wait_send()
        c_pa(k).wait_send()
        return 0

    lax.fori_loop(1, 8, drain_in, 0)

    def drain_gather(k, _):
        for d in (1, 3):
            c_gy(k, d).wait_send()
            c_gr(k, d).wait_send()
        c_gx(k).wait_send()
        c_gs(k).wait_send()
        c_gf(k).wait_send()
        return 0

    lax.fori_loop(0, 8, drain_gather, 0)

    def wait_ret(k, _):
        c_ra(k).wait_recv()
        c_rk(k).wait_recv()
        return 0

    lax.fori_loop(1, 8, wait_ret, 0)

    def unshuffle(t, q):
        return jnp.concatenate(
            [ret[h, t][:, q * 32:(q + 1) * 32] for h in range(8)], axis=-1
        )

    for q in range(8):
        rows = pl.ds(q * 64, 64)
        att = unshuffle(0, q).astype(F32)
        open_ = gate[rows, :]
        out = (open_ * att).astype(BF16)
        heads4[0, q] = out
        upd[q] = nn(out, ow[...]).astype(BF16)
        dpj[3, rows, :] = (gg[rows, :] * att * open_ * (1.0 - open_)).astype(BF16)
        for t in range(3):
            dpj[t, rows, :] = unshuffle(t + 1, q)
    put_upd = pltpu.make_async_copy(upd, upd_out, lsem.at[14])
    put_upd.start()
    for g in range(4):
        w = nn(nbt[...], dpj[g]).reshape(2, 8, 16, 256)
        ch[:, :, g * 16:(g + 1) * 16, :] = w
    w = tn(heads4[0].reshape(512, 256), ug[...].reshape(512, 256)).reshape(2, 8, 16, 256)
    ch[:, :, 64:80, :] = w

    ch[:, :, 80:96, :] = jnp.zeros((2, 8, 16, 256), F32)
    ch[0, 0, 80:88, 0:128] = pwacc[...]

    c_tc().start()
    c_tc().wait_recv()
    ch2[...] = (ch[c] + chr_[...]).astype(BF16)

    def start_ts(k, _):
        c_ts(k).start()
        return 0

    lax.fori_loop(1, 8, start_ts, 0)
    for q in range(8):
        rows = pl.ds(q * 64, 64)
        d = nt(dpj[0, rows, :], cw[:, 0:256])
        for g in range(1, 4):
            d += nt(dpj[g, rows, :], cw[:, g * 256:(g + 1) * 256])
        n = nf[rows, :]
        spread = spb[rows, 0:1]
        mean_d = jnp.mean(d, axis=-1, keepdims=True)
        mean_x = jnp.mean(d * n, axis=-1, keepdims=True)
        alg[q] = (spread * (d - mean_d - n * mean_x)).astype(BF16)
    put_alg = pltpu.make_async_copy(alg, alg_out, lsem.at[15])
    put_alg.start()

    def drain_out(k, _):
        for d in (1, 3):
            c_or(k, d).wait_send()
            c_oy(k, d).wait_send()
        c_os(k).wait_send()
        c_ox(k).wait_send()
        return 0

    lax.fori_loop(0, 8, drain_out, 0)

    def drain_ret(k, _):
        c_ra(k).wait_send()
        c_rk(k).wait_send()
        c_da(k).wait_send()
        return 0

    lax.fori_loop(1, 8, drain_ret, 0)
    for d in range(1, 4):
        c_py(d).wait_send()
        c_st(d).wait_send()
        c_dy(d).wait_send()
    for k in range(8):
        store(k).wait()
    put_upd.wait()
    put_alg.wait()
    acc = ch2[s].astype(F32)
    for k in range(1, 8):
        c_ts(k).wait_recv()
        acc += chs[k].astype(F32)
    chx[...] = acc.astype(BF16)
    chy[xh * 4 + y] = chx[...]

    def start_xy(m, _):
        c_txy(m).start()
        return 0

    lax.fori_loop(1, 8, start_xy, 0)
    for m in range(1, 8):
        c_txy(m).wait_recv()
    acc = chy[0].astype(F32)
    for a in range(1, 8):
        acc += chy[a].astype(F32)
    chf[c, s] = acc.astype(BF16)

    def start_as(k, _):
        c_as(k).start()
        return 0

    lax.fori_loop(1, 8, start_as, 0)
    for k in range(1, 8):
        c_as(k).wait_recv()
    c_ac().start()
    c_ac().wait_recv()

    put_sum = pltpu.make_async_copy(chf, chf_out, lsem.at[16])
    put_sum.start()

    def drain(k, _):
        c_ts(k).wait_send()
        c_as(k).wait_send()
        c_txy(k).wait_send()
        return 0

    lax.fori_loop(1, 8, drain, 0)
    c_tc().wait_send()
    c_ac().wait_send()
    put_sum.wait()


def finish(
    upd_in, alg_in, pg_in, chf_in, upd, alg, pg, dcw_out, dow_out, dpw_out,
    tok, pair, chf, dcw, dow, dpw, isem, osem,
):
    moves = [(pg_in.at[pl.ds(16 * a, 16)], pair.at[a], pg.at[pl.ds(16 * a, 16)]) for a in range(4)]
    moves.append((upd_in, tok.at[0], upd))
    moves.append((alg_in, tok.at[1], alg))
    first = pltpu.make_async_copy(chf_in, chf, isem.at[6])
    first.start()
    reads = [pltpu.make_async_copy(m[0], m[1], isem.at[i]) for i, m in enumerate(moves)]
    writes = [pltpu.make_async_copy(m[1], m[2], osem.at[i]) for i, m in enumerate(moves)]
    for copy in reads:
        copy.start()
    first.wait()
    for b in range(2):
        for q in range(8):
            at = (b * 8 + q) * 16
            for g in range(4):
                dcw[at:at + 16, g * 256:(g + 1) * 256] = chf[b, q, g * 16:(g + 1) * 16, :].astype(F32)
            dow[at:at + 16, :] = chf[b, q, 64:80, :].astype(F32)
    dpw[...] = chf[0, 0, 80:96, 0:128].astype(F32)[0:8]
    last = [
        pltpu.make_async_copy(dcw, dcw_out, osem.at[6]),
        pltpu.make_async_copy(dow, dow_out, osem.at[7]),
        pltpu.make_async_copy(dpw, dpw_out, osem.at[8]),
    ]
    for copy in last:
        copy.start()
    for read, write in zip(reads, writes):
        read.wait()
        write.start()
    for copy in writes + last:
        copy.wait()


def body(alignment_rows, pair_entries, combined_weight, output_weight, pair_weight, updated_gradient):
    V = pltpu.VMEM
    scratch = [
        V((512, 256), F32),
        V((512, 128), F32),
        V((512, 256), BF16),
        V((256, 512), BF16),
        V((512, 256), F32),
        V((512, 256), F32),
        V((4, 8, 64, 256), BF16),
        V((8, 4, 64, 256), BF16),
        V((8, 4, 2, 64, 256), BF16),
        V((8, 4, 2, 64, 256), BF16),
        V((8192, 128), F32),
        V((8192, 128), F32),
        V((8, 64, 128), F32),
        V((2, 4, 64, 128), F32),
        V((4, 2, 64, 128), F32),
        V((4, 256, 256), BF16),
        V((4, 8, 256), F32),
        V((256, 256), F32),
        V((256, 256), F32),
        V((8, 4, 2, 64, 256), BF16),
        V((8, 2, 2, 2, 64, 256), BF16),
        V((8, 4, 2, 64, 256), BF16),
        V((8, 2, 2, 64, 256), BF16),
        V((8, 2, 64, 256), BF16),
        V((8, 2, 64, 256), BF16),
        V((8, 4, 64, 256), BF16),
        V((8, 4, 64, 256), BF16),
        V((4, 2, 64, 128), F32),
        V((2, 4, 64, 128), F32),
        V((8, 64, 128), F32),
        V((4, 512, 256), BF16),
        V((2, 8, 96, 256), F32),
        V((8, 96, 256), F32),
        V((8, 96, 256), BF16),
        V((8, 96, 256), BF16),
        V((96, 256), BF16),
        V((8, 96, 256), BF16),
        V((8, 128), F32),
        V((8, 64, 256), BF16),
        V((64, 128, 128), BF16),
        V((256, 1024), BF16),
        V((256, 256), BF16),
        V((8, 128), F32),
        V((8, 64, 256), BF16),
        V((8, 64, 256), BF16),
        V((8, 64, 256), BF16),
        V((64, 128, 128), BF16),
        V((2, 8, 96, 256), BF16),
        pltpu.SemaphoreType.DMA((SEM_COUNT,)),
        pltpu.SemaphoreType.DMA((SEM_COUNT,)),
        pltpu.SemaphoreType.DMA((17,)),
    ]
    hbm = pl.BlockSpec(memory_space=pl.ANY)
    tokens = jax.ShapeDtypeStruct((8, 64, 256), BF16)
    pairs = jax.ShapeDtypeStruct((64, 128, 128), BF16)
    upd, alg, pg, chf = pl.pallas_call(
        kernel,
        out_shape=(tokens, tokens, pairs, jax.ShapeDtypeStruct((2, 8, 96, 256), BF16)),
        in_specs=[hbm] * 6,
        out_specs=(hbm,) * 4,
        scratch_shapes=scratch,
        compiler_params=pltpu.CompilerParams(
            collective_id=0, has_side_effects=True, vmem_limit_bytes=60 << 20
        ),
        name="row_attention",
    )(alignment_rows, pair_entries, combined_weight, output_weight, pair_weight.T, updated_gradient)
    done = pl.pallas_call(
        finish,
        out_shape=(
            tokens,
            tokens,
            pairs,
            jax.ShapeDtypeStruct((256, 1024), F32),
            jax.ShapeDtypeStruct((256, 256), F32),
            jax.ShapeDtypeStruct((8, 128), F32),
        ),
        in_specs=[hbm] * 4,
        out_specs=(hbm,) * 6,
        scratch_shapes=[
            V((2, 8, 64, 256), BF16),
            V((4, 16, 128, 128), BF16),
            V((2, 8, 96, 256), BF16),
            V((256, 1024), F32),
            V((256, 256), F32),
            V((8, 128), F32),
            pltpu.SemaphoreType.DMA((7,)),
            pltpu.SemaphoreType.DMA((9,)),
        ],
        compiler_params=pltpu.CompilerParams(vmem_limit_bytes=60 << 20),
        name="results",
    )(upd, alg, pg, chf)
    return *done[:5], done[5].T


def solution(mesh):
    return jax.shard_map(
        body,
        mesh=mesh,
        in_specs=(
            P("seq", "res", None),
            P("res", "seq", None),
            P(),
            P(),
            P(),
            P("seq", "res", None),
        ),
        out_specs=(
            P("seq", "res", None),
            P("seq", "res", None),
            P("res", "seq", None),
            P(),
            P(),
            P(),
        ),
        check_vma=False,
    )
```

```python
import math

import jax
import jax.numpy as jnp
from jax import lax
from jax.experimental import pallas as pl
from jax.experimental.pallas import tpu as pltpu
from jax.sharding import PartitionSpec as P

MESH = pl.DeviceIdType.MESH
EPS = 1e-05
SCALE = 1.0 / math.sqrt(2048)
F32 = jnp.float32
BF16 = jnp.bfloat16

IN_QA, IN_KV, GY, GX, GS, GF = 0, 8, 16, 48, 56, 64
PB_A, PB_Y, STAT = 72, 80, 84
OY, OS, OX, RT_A, RT_K = 88, 120, 128, 136, 144
DL_Y, DL_A = 152, 156
T_C, T_S, T_XY, T_AS, T_AC = 164, 165, 173, 181, 189
SEM_COUNT = 190
LAG = 3


def nt(a, b):
    return lax.dot_general(a, b, (((1,), (1,)), ((), ())), preferred_element_type=F32)


def tn(a, b):
    return lax.dot_general(a, b, (((0,), (0,)), ((), ())), preferred_element_type=F32)


def nn(a, b):
    return jnp.dot(a, b, preferred_element_type=F32)


def split2(v):
    hi = v.astype(BF16)
    lo = (v - hi.astype(F32)).astype(BF16)
    return hi, lo


def split3(v):
    hi = v.astype(BF16)
    rest = v - hi.astype(F32)
    mid = rest.astype(BF16)
    lo = (rest - mid.astype(F32)).astype(BF16)
    return hi, mid, lo


def kernel(
    al_in, pe_in, cw_in, ow_in, pw_in, ug_in,
    upd_out, alg_out, pg_out, chf_out,
    nf, spb, nb, nbt, gate, gg, heads4, sb, qa, kv,
    xn, rst, bs, pb, bi, bt, st, lt, dpt, oa, okv, ra, rsb, xb, rx, rb, ret,
    dl, dr, dx, dpj, ch, chr_, ch2, chs, chx, chy, pwacc,
    al, pe, cw, ow, pw, ug, upd, alg, pg, chf, ssem, rsem, lsem,
):
    s = lax.axis_index("seq")
    r = lax.axis_index("res")
    z, xl = s // 2, s % 2
    xh, y, c = r // 8, (r // 2) % 4, r % 2
    p = xh * 2 + c

    def at_seq(k):
        return {"seq": ((z + k // 2) % 4) * 2 + (xl + k) % 2}

    def from_seq(k):
        return {"seq": ((z + 4 - k // 2) % 4) * 2 + (xl + k) % 2}

    def at_y(d):
        return {"res": xh * 8 + ((y + d) % 4) * 2 + c}

    def at_xy(m):
        return {"res": ((xh + m // 4) % 2) * 8 + ((y + m) % 4) * 2 + c}

    at_x = {"res": (1 - xh) * 8 + y * 2 + c}
    at_c = {"res": xh * 8 + y * 2 + (1 - c)}

    def send(src, dst, i, where):
        return pltpu.make_async_remote_copy(
            src_ref=src, dst_ref=dst, send_sem=ssem.at[i], recv_sem=rsem.at[i],
            device_id=where, device_id_type=MESH,
        )

    loads = [
        pltpu.make_async_copy(a, b, lsem.at[8 + i])
        for i, (a, b) in enumerate(
            ((al_in, al), (cw_in, cw), (ug_in, ug), (ow_in, ow), (pw_in, pw), (pe_in, pe))
        )
    ]
    for load in loads:
        load.start()

    bar = pltpu.get_barrier_semaphore()
    for k in range(1, 8):
        pl.semaphore_signal(bar, inc=1, device_id=at_seq(k), device_id_type=MESH)
        pl.semaphore_signal(bar, inc=1, device_id=at_xy(k), device_id_type=MESH)
    pl.semaphore_signal(bar, inc=1, device_id=at_c, device_id_type=MESH)

    def c_in_qa(k):
        return send(sb.at[at_seq(k)["seq"], pl.ds(0, 2)], qa.at[k, y], IN_QA + k, at_seq(k))

    def c_in_kv(k):
        return send(sb.at[at_seq(k)["seq"], pl.ds(2, 2)], kv.at[k, p], IN_KV + k, at_seq(k))

    def c_gy(k, d):
        return send(qa.at[k, y], qa.at[k, y], GY + k * 4 + d, at_y(d))

    def c_gr(k, d):
        t = 0 if d == 1 else 1
        src = qa.at[k, (y + 4 - d) % 4, t]
        return send(src, src, GY + k * 4 + (0 if d == 1 else 2), at_y(d))

    def c_gx(k):
        return send(kv.at[k, p], kv.at[k, p], GX + k, at_x)

    def c_gs(k):
        return send(kv.at[k, p], kv.at[k, p], GS + k, at_c)

    px = (1 - xh) * 2 + c

    def c_gf(k):
        return send(kv.at[k, px], kv.at[k, px], GF + k, at_c)

    def c_pa(k):
        return send(bs.at[at_seq(k)["seq"]], pb.at[s // 4, s % 4], PB_A + k, at_seq(k))

    def c_py(d):
        return send(pb.at[:, (y + d) % 4], bi.at[y], PB_Y + d, at_y(d))

    def c_st(d):
        return send(st.at[y], st.at[y], STAT + d, at_y(d))

    def c_or(k, d):
        t = 0 if d == 1 else 1
        return send(
            oa.at[k, (y + 2) % 4, t], ra.at[k, 0 if d == 1 else 2, 0],
            OY + k * 4 + (0 if d == 1 else 2), at_y(d),
        )

    def c_oy(k, d):
        return send(oa.at[k, (y + d) % 4], ra.at[k, d], OY + k * 4 + d, at_y(d))

    def c_os(k):
        return send(okv.at[k, 1 - c], rsb.at[k], OS + k, at_c)

    def c_ox(k):
        return send(xb.at[k], rx.at[k], OX + k, at_x)

    def c_ra(k):
        return send(rb.at[k, pl.ds(0, 2)], ret.at[s, pl.ds(0, 2)], RT_A + k, from_seq(k))

    def c_rk(k):
        return send(rb.at[k, pl.ds(2, 2)], ret.at[s, pl.ds(2, 2)], RT_K + k, from_seq(k))

    def c_dy(d):
        return send(dl.at[(y + d) % 4], dr.at[:, y], DL_Y + d, at_y(d))

    def c_da(k):
        w = at_seq(k)["seq"]
        return send(dr.at[w // 4, w % 4], dx.at[s], DL_A + k, at_seq(k))

    def c_tc():
        return send(ch.at[1 - c], chr_, T_C, at_c)

    def c_ts(k):
        return send(ch2.at[at_seq(k)["seq"]], chs.at[k], T_S + k, at_seq(k))

    def c_txy(m):
        return send(chx, chy.at[xh * 4 + y], T_XY + m, at_xy(m))

    def c_as(k):
        return send(chf.at[c, s], chf.at[c, s], T_AS + k, at_seq(k))

    def c_ac():
        return send(chf.at[c], chf.at[c], T_AC, at_c)

    loads[0].wait()
    for q in range(8):
        x = al[q].astype(F32)
        cen = x - jnp.mean(x, axis=-1, keepdims=True)
        spread = lax.rsqrt(jnp.mean(cen * cen, axis=-1, keepdims=True) + EPS)
        normed = cen * spread
        rows = pl.ds(q * 64, 64)
        nf[rows, :] = normed
        spb[rows, :] = jnp.broadcast_to(spread, (64, 128))
        nb[rows, :] = normed.astype(BF16)
    def shuffle(t):
        for h in range(8):
            sb[h, t] = jnp.concatenate(
                [heads4[t, q][:, h * 32:(h + 1) * 32] for q in range(8)], axis=-1
            )

    for load in loads[1:4]:
        load.wait()
    for q in range(8):
        rows = pl.ds(q * 64, 64)
        n = nb[rows, :]
        heads4[0, q] = (nn(n, cw[:, 0:256]) * SCALE).astype(BF16)
        heads4[2, q] = nn(n, cw[:, 256:512]).astype(BF16)
        heads4[3, q] = nn(n, cw[:, 512:768]).astype(BF16)
        open_ = 1.0 / (1.0 + jnp.exp(-nn(n, cw[:, 768:1024])))
        gate[rows, :] = open_
        grad = nt(ug[q], ow[...])
        gg[rows, :] = grad
        heads4[1, q] = (grad * open_).astype(BF16)
    for h in range(8):
        for t in range(4):
            sb[h, t] = jnp.concatenate(
                [heads4[t, q][:, h * 32:(h + 1) * 32] for q in range(8)], axis=-1
            )
    pl.semaphore_wait(bar, 15)

    def start_in(k, _):
        c_in_kv(k).start()
        c_in_qa(k).start()
        return 0

    lax.fori_loop(1, 8, start_in, 0)
    qa[0, y] = sb[s, 0:2]
    kv[0, p] = sb[s, 2:4]
    c_gx(0).start()
    c_gs(0).start()
    for d in (1, 3):
        c_gy(0, d).start()

    for load in loads[4:]:
        load.wait()
    ones = jnp.ones((128, 128), BF16)
    w_all = pw[...]
    w3 = jnp.concatenate(split3(w_all), axis=0)

    def pair_chunk(k):
        base = pl.multiple_of(k * 1024, 1024)
        x = pe[pl.ds(k * 8, 8)].reshape(1024, 128)
        cen = x.astype(F32) - nn(x, ones) * (1.0 / 128)
        hi, lo = split2(cen * cen)
        spread = lax.rsqrt((nn(hi, ones) + nn(lo, ones)) * (1.0 / 128) + EPS)
        normed = cen * spread
        xn[pl.ds(base, 1024), :] = normed
        rst[pl.ds(base, 1024), :] = spread
        hi, lo = split2(normed)
        b = nt(w3, hi) + nt(w3, lo)
        b = b[0:8] + b[8:16] + b[16:24]
        for q in range(8):
            bs[:, k * 8 + q, :] = b[:, q * 128:(q + 1) * 128]

    def stage_in(k, _):
        c_in_kv(k).wait_recv()
        c_gx(k).start()
        c_gs(k).start()
        c_in_qa(k).wait_recv()
        for d in (1, 3):
            c_gy(k, d).start()
        pair_chunk(k)
        return 0

    lax.fori_loop(1, 8, stage_in, 0)
    pair_chunk(0)

    def start_pair(k, _):
        c_pa(k).start()
        return 0

    lax.fori_loop(1, 8, start_pair, 0)
    pb[s // 4, s % 4] = bs[s]

    def share_x(k, _):
        for d in (1, 3):
            c_gy(k, d).wait_recv()
            c_gr(k, d).start()
        c_gx(k).wait_recv()
        c_gf(k).start()
        return 0

    lax.fori_loop(0, 8, share_x, 0)
    nbt[...] = nb[...].T

    def wait_pair(k, _):
        c_pa(k).wait_recv()
        return 0

    lax.fori_loop(1, 8, wait_pair, 0)
    for d in range(1, 4):
        c_py(d).start()
    bi[y] = pb[:, y]

    dpt[...] = jnp.zeros_like(dpt)
    for d in range(1, 4):
        c_py(d).wait_recv()
    bias = jnp.concatenate(
        [jnp.concatenate([bi[a, b] for a in range(4)], axis=0) for b in range(2)], axis=1
    )
    lt[...] = bias.T

    def stage_mm(k, _):
        for d in (1, 3):
            c_gr(k, d).wait_recv()
        c_gs(k).wait_recv()
        c_gf(k).wait_recv()
        qk = qa[k, :, 0].reshape(256, 256)
        dak = qa[k, :, 1].reshape(256, 256)
        kk = kv[k, :, 0].reshape(256, 256)
        vk = kv[k, :, 1].reshape(256, 256)
        lt[...] += nt(kk, qk)
        dpt[...] += nt(vk, dak)
        return 0

    lax.fori_loop(0, 8, stage_mm, 0)
    logits = lt[...]
    top = jnp.max(logits, axis=0, keepdims=True)
    e = jnp.exp(logits - top)
    dp = dpt[...]
    total = jnp.sum(e, axis=0, keepdims=True)
    dots = jnp.sum(e * dp, axis=0, keepdims=True)
    st[y] = jnp.concatenate([top, total, dots, jnp.zeros((5, 256), F32)], axis=0)
    for d in range(1, 4):
        c_st(d).start()
    lt[...] = e
    for d in range(1, 4):
        c_st(d).wait_recv()
    stats = [st[a] for a in range(4)]
    peak = jnp.maximum(
        jnp.maximum(stats[0][0:1], stats[1][0:1]), jnp.maximum(stats[2][0:1], stats[3][0:1])
    )
    z_sum = jnp.zeros((1, 256), F32)
    d_sum = jnp.zeros((1, 256), F32)
    for a in range(4):
        f = jnp.exp(stats[a][0:1] - peak)
        z_sum += f * stats[a][1:2]
        d_sum += f * stats[a][2:3]
    inv = 1.0 / z_sum
    mine = st[y]
    prob_t = lt[...] * (jnp.exp(mine[0:1] - peak) * inv)
    grad_t = prob_t * (dpt[...] - d_sum * inv)
    lt[...] = prob_t
    dpt[...] = grad_t
    grad = grad_t.T
    for a in range(4):
        for b in range(2):
            dl[a, b] = grad[a * 64:(a + 1) * 64, b * 128:(b + 1) * 128]
    for d in range(1, 4):
        c_dy(d).start()
    dr[:, y] = dl[y]
    bt[0] = lt[...].astype(BF16)
    bt[1] = bt[0].T
    bt[2] = dpt[...].astype(BF16)
    bt[3] = grad.astype(BF16)

    def stage_out(k):
        qk = qa[k, :, 0].reshape(256, 256)
        dak = qa[k, :, 1].reshape(256, 256)
        kk = kv[k, :, 0].reshape(256, 256)
        vk = kv[k, :, 1].reshape(256, 256)
        dk = nn(bt[2], qk).astype(BF16)
        dv = nn(bt[0], dak).astype(BF16)
        for a in range(2):
            for b in range(2):
                at = (a * 2 + b) * 64
                okv[k, b, a, 0] = dk[at:at + 64]
                okv[k, b, a, 1] = dv[at:at + 64]
        c_os(k).start()
        oa[k, :, 0] = nn(bt[1], vk).astype(BF16).reshape(4, 64, 256)
        oa[k, :, 1] = (nn(bt[3], kk) * SCALE).astype(BF16).reshape(4, 64, 256)
        for d in (1, 3):
            c_or(k, d).start()

    def stage_y(k):
        for d in (1, 3):
            t = 0 if d == 1 else 1
            c_or(k, d).wait_recv()
            to = (y + d) % 4
            oa[k, to, t] = (
                oa[k, to, t].astype(F32) + ra[k, 0 if d == 1 else 2, 0].astype(F32)
            ).astype(BF16)
            c_oy(k, d).start()

    def stage_x(k):
        c_os(k).wait_recv()
        xb[k] = (okv[k, c, 1 - xh].astype(F32) + rsb[k, 1 - xh].astype(F32)).astype(BF16)
        c_ox(k).start()

    stage_out(1)

    def loop_out(i, _):
        stage_out((i + 1) % 8)
        stage_x(i)

        @pl.when(i > LAG)
        def _relay():
            stage_y(i - LAG)

        return 0

    lax.fori_loop(1, 8, loop_out, 0)
    stage_x(0)
    for i in range(8 - LAG, 9):
        stage_y(i % 8)

    for d in range(1, 4):
        c_dy(d).wait_recv()

    def start_da(k, _):
        c_da(k).start()
        return 0

    lax.fori_loop(1, 8, start_da, 0)
    dx[s] = dr[s // 4, s % 4]

    def wait_da(k, _):
        c_da(k).wait_recv()
        return 0

    lax.fori_loop(1, 8, wait_da, 0)
    w_mean = jnp.mean(w_all, axis=-1, keepdims=True)
    v_hi, v_mid, _ = split3(w_all - w_mean)
    one_rows = jnp.where(
        lax.broadcasted_iota(jnp.int32, (8, 128), 0) < 2, 1.0, 0.0
    ).astype(BF16)
    zero_rows = jnp.zeros((8, 128), BF16)
    rhs = jnp.concatenate(
        [
            jnp.concatenate([v_hi, zero_rows], axis=1),
            jnp.concatenate([v_mid, zero_rows], axis=1),
            jnp.concatenate([v_hi, zero_rows], axis=1),
            jnp.concatenate([zero_rows, one_rows], axis=1),
        ],
        axis=0,
    )
    pwacc[...] = jnp.zeros_like(pwacc)

    def store(k):
        rows = pl.ds(k * 8, 8)
        return pltpu.make_async_copy(pg.at[rows], pg_out.at[rows], lsem.at[k])

    def pair_back(k, _):
        base = pl.multiple_of(k * 1024, 1024)
        g = jnp.concatenate([dx[:, k * 8 + q, :] for q in range(8)], axis=1)
        b = jnp.concatenate([bs[:, k * 8 + q, :] for q in range(8)], axis=1)
        cross = jnp.sum(g * b, axis=0, keepdims=True) * (1.0 / 128)
        c_hi, c_lo = split2(cross)
        g_hi, g_lo = split2(g)
        tail = jnp.concatenate(
            [c_hi.astype(F32), c_lo.astype(F32), jnp.zeros((6, 1024), F32)], axis=0
        ).astype(BF16)
        lhs = jnp.concatenate([g_hi, g_hi, g_lo, tail], axis=0)
        both = tn(lhs, rhs)
        normed = xn[pl.ds(base, 1024), :]
        back = rst[pl.ds(base, 1024), :] * (both[:, 0:128] - normed * both[:, 128:256])
        pg[pl.ds(k * 8, 8)] = back.astype(BF16).reshape(8, 128, 128)
        store(k).start()
        n_hi, n_lo = split2(normed)
        g2 = jnp.concatenate([g_hi, g_lo], axis=0)
        part = nn(g2, n_hi) + nn(g2, n_lo)
        pwacc[...] += part[0:8] + part[8:16]
        return 0

    def sums(k):
        for d in (1, 3):
            c_oy(k, d).wait_recv()
        rb[k, 0:2] = (
            oa[k, y].astype(F32) + (ra[k, 1].astype(F32) + ra[k, 3].astype(F32))
        ).astype(BF16)
        c_ox(k).wait_recv()
        rb[k, 2:4] = (
            okv[k, c, xh].astype(F32) + rsb[k, xh].astype(F32) + rx[k].astype(F32)
        ).astype(BF16)

    def loop_sum(k, _):
        sums(k)
        c_ra(k).start()
        c_rk(k).start()
        return 0

    lax.fori_loop(1, 8, loop_sum, 0)
    sums(0)
    ret[s] = rb[0]
    lax.fori_loop(0, 8, pair_back, 0)

    def drain_in(k, _):
        c_in_qa(k).wait_send()
        c_in_kv(k).wait_send()
        c_pa(k).wait_send()
        return 0

    lax.fori_loop(1, 8, drain_in, 0)

    def drain_gather(k, _):
        for d in (1, 3):
            c_gy(k, d).wait_send()
            c_gr(k, d).wait_send()
        c_gx(k).wait_send()
        c_gs(k).wait_send()
        c_gf(k).wait_send()
        return 0

    lax.fori_loop(0, 8, drain_gather, 0)

    def wait_ret(k, _):
        c_ra(k).wait_recv()
        c_rk(k).wait_recv()
        return 0

    lax.fori_loop(1, 8, wait_ret, 0)

    def unshuffle(t, q):
        return jnp.concatenate(
            [ret[h, t][:, q * 32:(q + 1) * 32] for h in range(8)], axis=-1
        )

    for q in range(8):
        rows = pl.ds(q * 64, 64)
        att = unshuffle(0, q).astype(F32)
        open_ = gate[rows, :]
        out = (open_ * att).astype(BF16)
        heads4[0, q] = out
        upd[q] = nn(out, ow[...]).astype(BF16)
        dpj[3, rows, :] = (gg[rows, :] * att * open_ * (1.0 - open_)).astype(BF16)
        for t in range(3):
            dpj[t, rows, :] = unshuffle(t + 1, q)
    put_upd = pltpu.make_async_copy(upd, upd_out, lsem.at[14])
    put_upd.start()
    for g in range(4):
        w = nn(nbt[...], dpj[g]).reshape(2, 8, 16, 256)
        ch[:, :, g * 16:(g + 1) * 16, :] = w
    w = tn(heads4[0].reshape(512, 256), ug[...].reshape(512, 256)).reshape(2, 8, 16, 256)
    ch[:, :, 64:80, :] = w

    ch[:, :, 80:96, :] = jnp.zeros((2, 8, 16, 256), F32)
    ch[0, 0, 80:88, 0:128] = pwacc[...]

    c_tc().start()
    c_tc().wait_recv()
    ch2[...] = (ch[c] + chr_[...]).astype(BF16)

    def start_ts(k, _):
        c_ts(k).start()
        return 0

    lax.fori_loop(1, 8, start_ts, 0)
    for q in range(8):
        rows = pl.ds(q * 64, 64)
        d = nt(dpj[0, rows, :], cw[:, 0:256])
        for g in range(1, 4):
            d += nt(dpj[g, rows, :], cw[:, g * 256:(g + 1) * 256])
        n = nf[rows, :]
        spread = spb[rows, 0:1]
        mean_d = jnp.mean(d, axis=-1, keepdims=True)
        mean_x = jnp.mean(d * n, axis=-1, keepdims=True)
        alg[q] = (spread * (d - mean_d - n * mean_x)).astype(BF16)
    put_alg = pltpu.make_async_copy(alg, alg_out, lsem.at[15])
    put_alg.start()

    def drain_out(k, _):
        for d in (1, 3):
            c_or(k, d).wait_send()
            c_oy(k, d).wait_send()
        c_os(k).wait_send()
        c_ox(k).wait_send()
        return 0

    lax.fori_loop(0, 8, drain_out, 0)

    def drain_ret(k, _):
        c_ra(k).wait_send()
        c_rk(k).wait_send()
        c_da(k).wait_send()
        return 0

    lax.fori_loop(1, 8, drain_ret, 0)
    for d in range(1, 4):
        c_py(d).wait_send()
        c_st(d).wait_send()
        c_dy(d).wait_send()
    for k in range(8):
        store(k).wait()
    put_upd.wait()
    put_alg.wait()
    acc = ch2[s].astype(F32)
    for k in range(1, 8):
        c_ts(k).wait_recv()
        acc += chs[k].astype(F32)
    chx[...] = acc.astype(BF16)
    chy[xh * 4 + y] = chx[...]

    def start_xy(m, _):
        c_txy(m).start()
        return 0

    lax.fori_loop(1, 8, start_xy, 0)
    for m in range(1, 8):
        c_txy(m).wait_recv()
    acc = chy[0].astype(F32)
    for a in range(1, 8):
        acc += chy[a].astype(F32)
    chf[c, s] = acc.astype(BF16)

    def start_as(k, _):
        c_as(k).start()
        return 0

    lax.fori_loop(1, 8, start_as, 0)
    for k in range(1, 8):
        c_as(k).wait_recv()
    c_ac().start()
    c_ac().wait_recv()

    put_sum = pltpu.make_async_copy(chf, chf_out, lsem.at[16])
    put_sum.start()

    def drain(k, _):
        c_ts(k).wait_send()
        c_as(k).wait_send()
        c_txy(k).wait_send()
        return 0

    lax.fori_loop(1, 8, drain, 0)
    c_tc().wait_send()
    c_ac().wait_send()
    put_sum.wait()


def finish(
    upd_in, alg_in, pg_in, chf_in, upd, alg, pg, dcw_out, dow_out, dpw_out,
    tok, pair, chf, dcw, dow, dpw, isem, osem,
):
    moves = [(pg_in.at[pl.ds(16 * a, 16)], pair.at[a], pg.at[pl.ds(16 * a, 16)]) for a in range(4)]
    moves.append((upd_in, tok.at[0], upd))
    moves.append((alg_in, tok.at[1], alg))
    first = pltpu.make_async_copy(chf_in, chf, isem.at[6])
    first.start()
    reads = [pltpu.make_async_copy(m[0], m[1], isem.at[i]) for i, m in enumerate(moves)]
    writes = [pltpu.make_async_copy(m[1], m[2], osem.at[i]) for i, m in enumerate(moves)]
    for copy in reads:
        copy.start()
    first.wait()
    for b in range(2):
        for q in range(8):
            at = (b * 8 + q) * 16
            for g in range(4):
                dcw[at:at + 16, g * 256:(g + 1) * 256] = chf[b, q, g * 16:(g + 1) * 16, :].astype(F32)
            dow[at:at + 16, :] = chf[b, q, 64:80, :].astype(F32)
    dpw[...] = chf[0, 0, 80:96, 0:128].astype(F32)[0:8]
    last = [
        pltpu.make_async_copy(dcw, dcw_out, osem.at[6]),
        pltpu.make_async_copy(dow, dow_out, osem.at[7]),
        pltpu.make_async_copy(dpw, dpw_out, osem.at[8]),
    ]
    for copy in last:
        copy.start()
    for read, write in zip(reads, writes):
        read.wait()
        write.start()
    for copy in writes + last:
        copy.wait()


def body(alignment_rows, pair_entries, combined_weight, output_weight, pair_weight, updated_gradient):
    V = pltpu.VMEM
    scratch = [
        V((512, 256), F32),
        V((512, 128), F32),
        V((512, 256), BF16),
        V((256, 512), BF16),
        V((512, 256), F32),
        V((512, 256), F32),
        V((4, 8, 64, 256), BF16),
        V((8, 4, 64, 256), BF16),
        V((8, 4, 2, 64, 256), BF16),
        V((8, 4, 2, 64, 256), BF16),
        V((8192, 128), F32),
        V((8192, 128), F32),
        V((8, 64, 128), F32),
        V((2, 4, 64, 128), F32),
        V((4, 2, 64, 128), F32),
        V((4, 256, 256), BF16),
        V((4, 8, 256), F32),
        V((256, 256), F32),
        V((256, 256), F32),
        V((8, 4, 2, 64, 256), BF16),
        V((8, 2, 2, 2, 64, 256), BF16),
        V((8, 4, 2, 64, 256), BF16),
        V((8, 2, 2, 64, 256), BF16),
        V((8, 2, 64, 256), BF16),
        V((8, 2, 64, 256), BF16),
        V((8, 4, 64, 256), BF16),
        V((8, 4, 64, 256), BF16),
        V((4, 2, 64, 128), F32),
        V((2, 4, 64, 128), F32),
        V((8, 64, 128), F32),
        V((4, 512, 256), BF16),
        V((2, 8, 96, 256), F32),
        V((8, 96, 256), F32),
        V((8, 96, 256), BF16),
        V((8, 96, 256), BF16),
        V((96, 256), BF16),
        V((8, 96, 256), BF16),
        V((8, 128), F32),
        V((8, 64, 256), BF16),
        V((64, 128, 128), BF16),
        V((256, 1024), BF16),
        V((256, 256), BF16),
        V((8, 128), F32),
        V((8, 64, 256), BF16),
        V((8, 64, 256), BF16),
        V((8, 64, 256), BF16),
        V((64, 128, 128), BF16),
        V((2, 8, 96, 256), BF16),
        pltpu.SemaphoreType.DMA((SEM_COUNT,)),
        pltpu.SemaphoreType.DMA((SEM_COUNT,)),
        pltpu.SemaphoreType.DMA((17,)),
    ]
    hbm = pl.BlockSpec(memory_space=pl.ANY)
    tokens = jax.ShapeDtypeStruct((8, 64, 256), BF16)
    pairs = jax.ShapeDtypeStruct((64, 128, 128), BF16)
    upd, alg, pg, chf = pl.pallas_call(
        kernel,
        out_shape=(tokens, tokens, pairs, jax.ShapeDtypeStruct((2, 8, 96, 256), BF16)),
        in_specs=[hbm] * 6,
        out_specs=(hbm,) * 4,
        scratch_shapes=scratch,
        compiler_params=pltpu.CompilerParams(
            collective_id=0, has_side_effects=True, vmem_limit_bytes=60 << 20
        ),
        name="row_attention",
    )(alignment_rows, pair_entries, combined_weight, output_weight, pair_weight.T, updated_gradient)
    done = pl.pallas_call(
        finish,
        out_shape=(
            tokens,
            tokens,
            pairs,
            jax.ShapeDtypeStruct((256, 1024), F32),
            jax.ShapeDtypeStruct((256, 256), F32),
            jax.ShapeDtypeStruct((8, 128), F32),
        ),
        in_specs=[hbm] * 4,
        out_specs=(hbm,) * 6,
        scratch_shapes=[
            V((2, 8, 64, 256), BF16),
            V((4, 16, 128, 128), BF16),
            V((2, 8, 96, 256), BF16),
            V((256, 1024), F32),
            V((256, 256), F32),
            V((8, 128), F32),
            pltpu.SemaphoreType.DMA((7,)),
            pltpu.SemaphoreType.DMA((9,)),
        ],
        compiler_params=pltpu.CompilerParams(vmem_limit_bytes=60 << 20),
        name="results",
    )(upd, alg, pg, chf)
    return *done[:5], done[5].T


def solution(mesh):
    return jax.shard_map(
        body,
        mesh=mesh,
        in_specs=(
            P("seq", "res", None),
            P("res", "seq", None),
            P(),
            P(),
            P(),
            P("seq", "res", None),
        ),
        out_specs=(
            P("seq", "res", None),
            P("seq", "res", None),
            P("res", "seq", None),
            P(),
            P(),
            P(),
        ),
        check_vma=False,
    )
```
